32 devices in a mesh: tm: 4 (over x, core), sensor: 8 (over z, y).
Axes of the slice: x: 2, y: 2, z: 4, core: 2. Of those that a mesh axis runs over, the one named last changes fastest.
Arguments:
- values: bfloat16 [65536, 256], P('sensor'), may hold values from -0.046875 to 0.046875
- blocks: int32 [65536, 2], P('sensor'), may hold values from 0 to 7, all different within a row
- noise_scale: float32 [4, 65536], P('tm', 'sensor'), may hold values from 0.5 to 2
- readings: float32 [4, 65536], P('tm', 'sensor'), may hold values from -6 to 6
- available: int32 [4, 65536], P('tm', 'sensor'), may hold values 0 or 1
- decay: float32 [4, 1024], P('tm'), may hold values from 0.7 to 1
- prior_factor: float32 [1024, 1024], replicated, may hold values from -3 to 3, as said below
- prior_target: float32 [1024], replicated, may hold values from -6 to 6
Outputs:
- factor_post: float32 [4, 1024, 1024], P('tm', 'sensor')
- estimate: float32 [4, 1024], P('tm')
The draws below stay inside these ranges and needn't reach their ends.
Inputs may be any that keep to these rules, and one draw needn't show every extreme that they name: `prior_factor`: upper triangular; diagonal entries from 1 to 3, the other upper entries at most 3 / sqrt(1024) in size.
All inputs are finite; a program needn't handle non-finite values. No bound on the sum of `available` on one device may be relied on, other than what follows from the above.
Results may differ from the reference program's by a relative error of at most 0.0038.
Values sent between devices are 32-bit elements; how exact they have to be, the bound alone decides.
No kernel may reach another device: no remote copies, remote signals or barrier semaphores. Data moves between devices by JAX's collectives and lax.ppermute only.
A program may use at most 128 MiB of HBM per device.

```python
import math
import jax
import jax.numpy as jnp
from jax import lax

NS = 1024
BLK = 128
NBLK = 8
ROWS_DEV = 8192
ROWS = 65536
STEPS = 4
N_SENSOR = 8


def draw_prior_factor(key, part):
    key = jax.random.fold_in(key, 7)
    key_diag, key_off = jax.random.split(key)
    row_ids = jnp.arange(NS, dtype=jnp.int32)[:, None]
    col_ids = jnp.arange(NS, dtype=jnp.int32)[None, :]
    diagonal = jax.random.uniform(key_diag, (NS,), jnp.float32, 1.0, 2.0)
    upper = jax.random.truncated_normal(key_off, -3.0, 3.0, (NS, NS), jnp.float32) / jnp.sqrt(jnp.float32(NS))
    result = jnp.where(col_ids > row_ids, upper, 0.0) + jnp.where(col_ids == row_ids, diagonal[None, :], 0.0)
    return result.astype(jnp.float32)


def plant(values, own_key, smallest, high):
    longest = values.shape.index(max(values.shape))
    spots = []
    for shift in (0, 1):
        where = [jax.random.randint(jax.random.fold_in(own_key, axis), (), 0, length) for axis, length in enumerate(values.shape)]
        where[longest] = (where[longest] + shift) % values.shape[longest]
        spots.append(tuple(where))
    return values.at[spots[0]].set(smallest).at[spots[1]].set(high)


def block_scale(own_key, extent, cuts, least, largest):
    def one(position, shards_of):
        heights = jax.random.uniform(jax.random.fold_in(jax.random.fold_in(own_key, 6), position), (shards_of,), jnp.float32, least / len(cuts), largest / len(cuts))
        return jnp.repeat(jnp.exp(heights), extent[position] // shards_of).reshape((-1,) + (1,) * (len(extent) - position - 1))

    factor_of = one(*cuts[0])
    for cut in cuts[1:]:
        factor_of = factor_of * one(*cut)
    return factor_of


def choose_distinct(key, rows, amount, top, lift):
    sequence = jax.random.permutation(jax.random.fold_in(key, 1), amount)
    pull = sequence
    for power in range(3):
        pull = pull * pull // amount
    pull = pull * lift // amount
    chance = jax.random.randint(jax.random.fold_in(key, 2), (rows, amount), 0, 4096) + pull
    holders = jax.random.permutation(jax.random.fold_in(key, 3), rows)[jnp.arange(amount) % rows]
    chance = jnp.where(jnp.arange(rows)[:, None] == holders[None, :], 1 << 14, chance)
    merit = chance * amount + jnp.arange(amount)
    return lax.top_k(merit.astype(jnp.int32), top)[1].astype(jnp.int32)


def noise(rng, extent, scale, limit, cuts=(), kind=jnp.bfloat16):
    values = jax.random.normal(rng, extent, jnp.float32) * scale
    if len(cuts) > 0:
        values = block_scale(rng, extent, cuts, -0.22, 0.18) * values
    return jnp.clip(values, min=-limit, max=limit).astype(kind)


def setup_inputs(seed: int = 0) -> dict:
    seeds = jax.random.split(jax.random.key(seed), 9)
    values = noise(seeds[0], (ROWS, 2 * BLK), (2.0 / (ROWS_DEV * N_SENSOR) ** 0.5), 0.046875, ((0, 8),))
    blocks = choose_distinct(seeds[1], ROWS, NBLK, 2, 0)
    noise_scale = jnp.clip(jnp.exp(math.log(2.0) - 1.3862944 * jax.random.uniform(seeds[2], (STEPS, ROWS), jnp.float32) ** block_scale(seeds[2], (STEPS, ROWS), ((0, 4), (1, 8)), -0.2, 0.2)), 0.5, 2.0)
    readings = noise(seeds[3], (STEPS, ROWS), 1.0, 6.0, ((0, 4), (1, 8)), jnp.float32)
    available = plant((jax.random.randint(seeds[4], (STEPS, ROWS), 0, 5) < 4).astype(jnp.int32), jax.random.fold_in(seeds[4], 1), 0, 1)
    decay = jnp.clip(jnp.exp(math.log(1.0) - 0.35667496 * jax.random.uniform(seeds[5], (STEPS, NS), jnp.float32) ** block_scale(seeds[5], (STEPS, NS), ((0, 4),), -0.2, 0.2)), 0.7, 1.0)
    prior_factor = draw_prior_factor(jax.random.fold_in(seeds[8], 71), 0)
    prior_target = noise(seeds[7], (NS,), 1.0, 6.0, (), jnp.float32)
    return dict(values=values, blocks=blocks, noise_scale=noise_scale, readings=readings, available=available, decay=decay, prior_factor=prior_factor, prior_target=prior_target)


def expand(weighted, blocks, count):
    width = weighted.shape[1] // 2
    picked = (blocks[:, :, None] == jnp.arange(count, dtype=jnp.int32)[None, None, :]).astype(weighted.dtype)
    first = weighted[:, :width]
    second = weighted[:, width:]
    dense = picked[:, 0, :, None] * first[:, None, :] + picked[:, 1, :, None] * second[:, None, :]
    return dense.reshape(weighted.shape[0], count * width)

def whiten(values, noise_row, reading_row, avail_row):
    factor = avail_row.astype(jnp.float32) / noise_row
    weighted = (values.astype(jnp.float32) * factor[:, None]).astype(jnp.bfloat16)
    target = (reading_row * factor).astype(jnp.bfloat16)
    return (weighted, target)

def reference(values, blocks, noise_scale, readings, available, decay, prior_factor, prior_target):
    count = NS // BLK
    width_full = NS
    value_parts = values.reshape(N_SENSOR, ROWS_DEV, values.shape[1])
    block_parts = blocks.reshape(N_SENSOR, ROWS_DEV, 2)

    def accumulate(carry, piece):
        vals, blks, noise_row, reading_row, avail_row = piece
        weighted, target = whiten(vals, noise_row, reading_row, avail_row)
        dense = expand(weighted, blks, count).astype(jnp.float32)
        gram_part = jnp.dot(dense.T.astype(jnp.float32), dense.astype(jnp.float32), precision=lax.Precision.HIGHEST, preferred_element_type=jnp.float32)
        vec_part = jnp.dot(target.astype(jnp.float32), dense.astype(jnp.float32), precision=lax.Precision.HIGHEST, preferred_element_type=jnp.float32)
        return ((carry[0] + gram_part, carry[1] + vec_part), None)
    info_now = jnp.dot(prior_factor.T.astype(jnp.float32), prior_factor.astype(jnp.float32), precision=lax.Precision.HIGHEST, preferred_element_type=jnp.float32)
    ivec_now = jnp.dot(prior_target.astype(jnp.float32), prior_factor.astype(jnp.float32), precision=lax.Precision.HIGHEST, preferred_element_type=jnp.float32)
    factors = []
    estimates = []
    for step_index in range(STEPS):
        start = (jnp.zeros((width_full, width_full), jnp.float32), jnp.zeros((width_full,), jnp.float32))
        pieces = (value_parts, block_parts, noise_scale[step_index].reshape(N_SENSOR, ROWS_DEV), readings[step_index].reshape(N_SENSOR, ROWS_DEV), available[step_index].reshape(N_SENSOR, ROWS_DEV))
        (gram_total, vec_total), unused = lax.scan(accumulate, start, pieces)
        post = info_now + gram_total
        pvec = ivec_now + vec_total
        lower = jnp.linalg.cholesky(post)
        middle = lax.linalg.triangular_solve(lower, pvec[:, None], left_side=True, lower=True)
        solved = lax.linalg.triangular_solve(lower, middle, left_side=True, lower=True, transpose_a=True)
        factors.append(lower.T)
        estimates.append(solved[:, 0])
        rate = decay[step_index]
        info_now = rate[:, None] * post * rate[None, :]
        ivec_now = rate * pvec
    return (jnp.stack(factors), jnp.stack(estimates))
```

```python
import functools

import jax
import jax.numpy as jnp
from jax import lax
from jax.experimental import pallas as pl
from jax.experimental.pallas import tpu as pltpu
from jax.sharding import PartitionSpec as P

HI = lax.Precision.HIGHEST
SUB = 8
CHUNK = 1024
BF16 = jnp.bfloat16
F32 = jnp.float32


def block_row(i, j, count):
    return i * count - i * (i - 1) // 2 + (j - i)


def packed_rows(count, width, sensors):
    return count * (count + 1) // 2 * width + SUB * sensors


def column_of(row):
    n = row.shape[1]
    return jnp.broadcast_to(row, (n, n)).T


def nt(a, b):
    return lax.dot_general(a, b, (((1,), (1,)), ((), ())), preferred_element_type=F32)


def gram_kernel(
    count, v_ref, b_ref, n_ref, r_ref, a_ref, p_ref, t_ref, out_ref, wide_ref, vec_ref, *acc_refs
):
    step = pl.program_id(0)
    width = v_ref.shape[1] // 2
    pair = 2 * width
    chunk = v_ref.shape[0]

    @pl.when(step == 0)
    def _():
        vec_ref[...] = jnp.zeros_like(vec_ref)
        for acc in acc_refs:
            acc[...] = jnp.zeros_like(acc)

    factor = a_ref[...].astype(F32) / n_ref[...]
    target = jnp.broadcast_to(r_ref[...] * factor, (16, chunk)).astype(BF16)
    rows = lax.broadcasted_iota(jnp.int32, (pair, pair), 0)
    cols = lax.broadcasted_iota(jnp.int32, (pair, pair), 1)
    eye = (rows == cols).astype(F32).astype(BF16)
    weighted = (nt(eye, v_ref[...]) * factor).astype(BF16)
    blocks = b_ref[...]
    for b in range(count):
        hit = jnp.where(blocks == b, 1.0, 0.0)
        hit0 = jnp.broadcast_to(hit[0:1], (16, chunk)).astype(BF16)
        hit1 = jnp.broadcast_to(hit[1:2], (16, chunk)).astype(BF16)
        for q in range(width // 16):
            lo = 16 * q
            wide_ref[b * width + lo : b * width + lo + 16, :] = (
                weighted[lo : lo + 16] * hit0 + weighted[width + lo : width + lo + 16] * hit1
            )
    for j, acc in enumerate(acc_refs):
        right = wide_ref[j * pair : (j + 1) * pair, :]
        acc[...] += nt(wide_ref[0 : (j + 1) * pair, :], right)
        vec_ref[:, j * pair : (j + 1) * pair] += nt(target, right)

    @pl.when(step == pl.num_programs(0) - 1)
    def _():
        prior = p_ref[...]
        vec = vec_ref[0:1, :] + jnp.dot(t_ref[...], prior, precision=HI, preferred_element_type=F32)
        base = count * (count + 1) // 2 * width
        out_ref[base:, :] = jnp.zeros((out_ref.shape[0] - base, width), F32)
        for i in range(count):
            out_ref[base + i : base + i + 1, :] = vec[:, i * width : (i + 1) * width]
        for j, acc in enumerate(acc_refs):
            total = acc[...] + lax.dot_general(
                prior[:, : (j + 1) * pair],
                prior[:, j * pair : (j + 1) * pair],
                (((0,), (0,)), ((), ())),
                precision=HI,
                preferred_element_type=F32,
            )
            for jj in (2 * j, 2 * j + 1):
                for i in range(jj + 1):
                    at = block_row(i, jj, count) * width
                    out_ref[at : at + width, :] = total[
                        i * width : (i + 1) * width, (jj % 2) * width : (jj % 2 + 1) * width
                    ]


def local_gram(values, blocks, noise, reading, avail, prior, target, count, sensors):
    rows, pair = values.shape
    width = pair // 2
    states = count * width
    total = packed_rows(count, width, sensors)
    line = pl.BlockSpec((1, CHUNK), lambda c: (0, c))
    whole = lambda shape: pl.BlockSpec(shape, lambda c: (0,) * len(shape))
    return pl.pallas_call(
        functools.partial(gram_kernel, count),
        grid=(rows // CHUNK,),
        in_specs=[
            pl.BlockSpec((CHUNK, pair), lambda c: (c, 0)),
            pl.BlockSpec((2, CHUNK), lambda c: (0, c)),
            line,
            line,
            line,
            whole(prior.shape),
            whole(target.shape),
        ],
        out_specs=whole((total, width)),
        out_shape=jax.ShapeDtypeStruct((total, width), F32),
        scratch_shapes=[pltpu.VMEM((states, CHUNK), BF16), pltpu.VMEM((16, states), F32)]
        + [pltpu.VMEM(((j + 1) * pair, pair), F32) for j in range(states // pair)],
        compiler_params=pltpu.CompilerParams(vmem_limit_bytes=48 << 20),
        cost_estimate=pl.CostEstimate(
            flops=2 * rows * states * states * 5 // 8, bytes_accessed=rows * pair * 2, transcendentals=0
        ),
        name="gram",
    )(values, blocks, noise, reading, avail, prior, target)


def frame_kernel(count, f_ref, out_ref):
    width = out_ref.shape[1]
    base = count * (count + 1) // 2 * width
    out_ref[base:, :] = jnp.zeros((out_ref.shape[0] - base, width), F32)
    parts = [f_ref[:, i * width : (i + 1) * width] for i in range(count)]
    for i in range(count):
        out_ref[base + i : base + i + 1, :] = parts[i]
        column = column_of(parts[i])
        for j in range(i, count):
            at = block_row(i, j, count) * width
            out_ref[at : at + width, :] = column * parts[j]


def frame_scale(inverse, count, width, sensors):
    total = packed_rows(count, width, sensors)
    return pl.pallas_call(
        functools.partial(frame_kernel, count),
        out_shape=jax.ShapeDtypeStruct((total, width), F32),
        cost_estimate=pl.CostEstimate(flops=total * width, bytes_accessed=total * width * 4, transcendentals=0),
        name="frames",
    )(inverse)


def spread(x, index, axis):
    return jnp.broadcast_to(lax.slice_in_dim(x, index, index + 1, axis=axis), x.shape)


def split3(x):
    a = x.astype(BF16)
    rest = x - a.astype(F32)
    b = rest.astype(BF16)
    return a, b, (rest - b.astype(F32)).astype(BF16)


def far_product(top, both):
    a, b, c = split3(both)
    left = jnp.concatenate([a, a, b, a, c, b], 0)[:, : top.shape[1]]
    right = jnp.concatenate([a, b, a, c, a, b], 0)
    return lax.dot_general(left, right, (((0,), (0,)), ((), ())), preferred_element_type=F32)


def diag_factor(block):
    size = block.shape[0]
    groups = size // SUB
    lane = lax.broadcasted_iota(jnp.int32, (SUB, size), 1)
    sub = lax.broadcasted_iota(jnp.int32, (SUB, size), 0)
    left = [block[SUB * r : SUB * (r + 1), :] for r in range(groups)]
    right = [(lane == sub + SUB * r).astype(F32) for r in range(groups)]
    tops = []
    lows = []
    for g in range(groups):
        near = min(groups, g + 2)
        cols = {r: [spread(left[r], SUB * g + k, 1) for k in range(SUB)] for r in range(g, near)}
        s = [[spread(cols[g][k], i, 0) if i >= k else None for k in range(SUB)] for i in range(SUB)]
        xs = [spread(left[g], k, 0) for k in range(SUB)]
        ys = [spread(right[g], k, 0) for k in range(SUB)]
        inv = []
        for k in range(SUB):
            inv.append(lax.rsqrt(s[k][k]))
            for i in range(k + 1, SUB):
                s[i][k] = s[i][k] * inv[k]
            for j in range(k + 1, SUB):
                for i in range(j, SUB):
                    s[i][j] = s[i][j] - s[i][k] * s[j][k]
            xs[k] = xs[k] * inv[k]
            ys[k] = ys[k] * inv[k]
            for i in range(k + 1, SUB):
                xs[i] = xs[i] - s[i][k] * xs[k]
                ys[i] = ys[i] - s[i][k] * ys[k]
        for r in range(g + 1, near):
            ls = cols[r]
            for k in range(SUB):
                ls[k] = ls[k] * inv[k]
                for j in range(k + 1, SUB):
                    ls[j] = ls[j] - s[j][k] * ls[k]
                left[r] = left[r] - ls[k] * xs[k]
                right[r] = right[r] - ls[k] * ys[k]
        top, low = xs[0], ys[0]
        for k in range(1, SUB):
            top = jnp.where(sub == k, xs[k], top)
            low = jnp.where(sub == k, ys[k], low)
        if near < groups:
            delta = far_product(top, jnp.concatenate([top, low], 1))
            for r in range(near, groups):
                left[r] = left[r] - delta[SUB * r : SUB * (r + 1), :size]
                right[r] = right[r] - delta[SUB * r : SUB * (r + 1), size:]
        tops.append(jnp.where(lane >= sub + SUB * g, top, 0.0))
        lows.append(low)
    return jnp.concatenate(tops, 0), jnp.concatenate(lows, 0)


def dot_tn(a, b):
    return lax.dot_general(a, b, (((0,), (0,)), ((), ())), precision=HI, preferred_element_type=F32)


def dot_nn(a, b):
    return jnp.dot(a, b, precision=HI, preferred_element_type=F32)


def factor_kernel(count, own_ref, x_ref, f_ref, rows_ref, est_ref, s_ref, r_ref, t_ref):
    width = x_ref.shape[1]
    share = rows_ref.shape[0]
    base = count * (count + 1) // 2 * width

    def prior_row(k):
        parts = []
        for j in range(k, count):
            at = block_row(k, j, count) * width
            parts.append(x_ref[at : at + width, :])
        parts.append(column_of(x_ref[base + k : base + k + 1, :]))
        return jnp.concatenate(parts, 1)

    s_ref[:, :] = prior_row(0)

    @pl.loop(0, count)
    def _(k):
        at = pl.multiple_of(k * width, width)
        upper, inverse = diag_factor(s_ref[:, pl.ds(at, width)])
        t_ref[pl.ds(at, width), :] = inverse
        r_ref[pl.ds(at, width), pl.ds(at, width)] = upper
        for kk in range(count):

            @pl.when(k == kk)
            def _():
                rest = (kk + 1) * width
                row = dot_nn(t_ref[kk * width : rest, :], s_ref[:, rest:])
                r_ref[kk * width : rest, rest:] = row
                if kk + 1 < count:
                    s_ref[:, rest:] = prior_row(kk + 1) - dot_tn(
                        r_ref[0:rest, rest : rest + width], r_ref[0:rest, rest:]
                    )

    states = count * width
    solved = [None] * count
    for k in reversed(range(count)):
        right = r_ref[k * width : (k + 1) * width, states:]
        if k + 1 < count:
            right = right - dot_nn(
                r_ref[k * width : (k + 1) * width, (k + 1) * width : states],
                jnp.concatenate(solved[k + 1 :], 0),
            )
        solved[k] = dot_tn(t_ref[k * width : (k + 1) * width, :], right)
    for k in range(count):
        cols = slice(k * width, (k + 1) * width)
        est_ref[:, cols] = solved[k].T[0:1, :] / f_ref[:, cols]
    first = pl.multiple_of(own_ref[0] * share, share)
    for j in range(count):
        cols = slice(j * width, (j + 1) * width)
        mine = r_ref[pl.ds(first, share), cols] * f_ref[:, cols]
        rows_ref[:, cols] = jnp.where(first < (j + 1) * width, mine, 0.0)


def factor(own, packed, frame, count, share):
    width = packed.shape[1]
    states = count * width
    vmem = pl.BlockSpec(memory_space=pltpu.VMEM)
    return pl.pallas_call(
        functools.partial(factor_kernel, count),
        in_specs=[pl.BlockSpec(memory_space=pltpu.SMEM), vmem, vmem],
        out_specs=[vmem, vmem],
        out_shape=[
            jax.ShapeDtypeStruct((share, states), F32),
            jax.ShapeDtypeStruct((1, states), F32),
        ],
        scratch_shapes=[
            pltpu.VMEM((width, states + width), F32),
            pltpu.VMEM((states, states + width), F32),
            pltpu.VMEM((states, width), F32),
        ],
        compiler_params=pltpu.CompilerParams(vmem_limit_bytes=48 << 20),
        cost_estimate=pl.CostEstimate(
            flops=4 * states**3, bytes_accessed=packed.size * 4, transcendentals=states
        ),
        name="factor",
    )(own, packed, frame)


def per_device(values, blocks, noise_scale, readings, available, decay, prior_factor, prior_target):
    states = prior_factor.shape[0]
    width = values.shape[1] // 2
    count = states // width
    sensors = lax.axis_size("sensor")
    steps = lax.axis_size("tm")
    share = states // sensors
    own = lax.axis_index("sensor")
    time = lax.axis_index("tm")

    def earlier(x, by):
        return lax.ppermute(x, "tm", [(i, i + by) for i in range(steps - by)])

    frame = jnp.ones((1, states), F32)
    for by in range(1, steps):
        frame = frame * jnp.where(time >= by, earlier(decay, by), 1.0)
    first = (time == 0).astype(F32)
    prior = lax.dynamic_slice_in_dim(prior_factor, own * share, share, 0) * first
    target = lax.dynamic_slice_in_dim(prior_target, own * share, share, 0)[None, :]
    packed = local_gram(
        values, blocks.T, noise_scale, readings, available, prior, target, count, sensors
    )
    scale = frame_scale(1.0 / frame, count, width, sensors)
    piece = packed.shape[0] // sensors
    scale = lax.dynamic_slice_in_dim(scale, own * piece, piece, 0)
    part = lax.psum_scatter(packed, "sensor", scatter_dimension=0, tiled=True) * scale
    by = 1
    while by < steps:
        part = part + earlier(part, by)
        by *= 2
    packed = lax.all_gather(part, "sensor", axis=0, tiled=True)
    rows, estimate = factor(own.astype(jnp.int32)[None], packed, frame, count, share)
    return rows[None], estimate


def solution(mesh):
    placed = (
        P("sensor", None),
        P("sensor", None),
        P("tm", "sensor"),
        P("tm", "sensor"),
        P("tm", "sensor"),
        P("tm", None),
        P(),
        P(),
    )
    return jax.shard_map(
        per_device,
        mesh=mesh,
        in_specs=placed,
        out_specs=(P("tm", "sensor", None), P("tm", None)),
        check_vma=False,
    )
```

```python
import functools

import jax
import jax.numpy as jnp
from jax import lax
from jax.experimental import pallas as pl
from jax.experimental.pallas import tpu as pltpu
from jax.sharding import PartitionSpec as P

HI = lax.Precision.HIGHEST
SUB = 8
CHUNK = 2048
VMEM_BYTES = 60 << 20
CUTS = (2, 4)
CUT_PLACES = (0,) + CUTS
FAR = 2
FACTOR_FLOPS = 5 * 10**9
BF16 = jnp.bfloat16
F32 = jnp.float32


def upper_blocks(lo, hi, count):
    return [(i, j) for i in range(lo, hi) for j in range(i, count)]


def column_of(row):
    n = row.shape[1]
    return jnp.broadcast_to(row, (n, n)).T


def nt(a, b):
    return lax.dot_general(a, b, (((1,), (1,)), ((), ())), preferred_element_type=F32)


def dot_tn(a, b):
    return lax.dot_general(a, b, (((0,), (0,)), ((), ())), precision=HI, preferred_element_type=F32)


def dot_nn(a, b):
    return jnp.dot(a, b, precision=HI, preferred_element_type=F32)


def tiles(lo, hi, count):
    spans = [(j, min(j + 2, count)) for j in range(lo, count, 2)]
    return [(first, end, min(end, hi)) for first, end in spans]


def gram_kernel(
    count, spans, place_ref, v_ref, b_ref, n_ref, r_ref, a_ref, p_ref, t_ref, *refs
):
    out_refs = refs[: 2 * len(spans)]
    packed_refs = refs[2 * len(spans) : 3 * len(spans)]
    wide_ref, *acc_refs = refs[3 * len(spans) :]
    lo, hi = spans[0][0], spans[-1][1]
    step = pl.program_id(0)
    width = v_ref.shape[1] // 2
    pair = 2 * width
    chunk = v_ref.shape[0]
    top = 16 if lo == 0 else 0

    @pl.when(step == 0)
    def _():
        for acc in acc_refs:
            acc[...] = jnp.zeros_like(acc)

    factor = a_ref[...].astype(F32) / n_ref[...]
    if top:
        wide_ref[0:top, :] = jnp.broadcast_to(r_ref[...] * factor, (top, chunk)).astype(BF16)
    rows = lax.broadcasted_iota(jnp.int32, (pair, pair), 0)
    cols = lax.broadcasted_iota(jnp.int32, (pair, pair), 1)
    eye = (rows == cols).astype(F32).astype(BF16)
    weighted = (nt(eye, v_ref[...]) * factor).astype(BF16)
    blocks = b_ref[...]
    for b in range(lo, count):
        hit = jnp.where(blocks == b, 1.0, 0.0)
        hit0 = jnp.broadcast_to(hit[0:1], (16, chunk)).astype(BF16)
        hit1 = jnp.broadcast_to(hit[1:2], (16, chunk)).astype(BF16)
        for q in range(0, width, 16):
            at = top + (b - lo) * width + q
            wide_ref[at : at + 16, :] = (
                weighted[q : q + 16] * hit0 + weighted[width + q : width + q + 16] * hit1
            )
    columns = tiles(lo, hi, count)
    for (first, end, stop), acc in zip(columns, acc_refs):
        acc[...] += nt(
            wide_ref[0 : top + (stop - lo) * width, :],
            wide_ref[top + (first - lo) * width : top + (end - lo) * width, :],
        )

    @pl.when(step == pl.num_programs(0) - 1)
    def _():
        prior = p_ref[...] * place_ref[1].astype(F32)
        totals = [
            acc[top:, :]
            + dot_tn(prior[:, lo * width : stop * width], prior[:, first * width : end * width])
            for (first, end, stop), acc in zip(columns, acc_refs)
        ]
        for n, (start, past) in enumerate(spans):
            kept = upper_blocks(start, past, count)
            packed_ref = packed_refs[n]
            for m, (i, j) in enumerate(kept):
                tile = (j - lo) // 2
                across = j - columns[tile][0]
                packed_ref[m * width : (m + 1) * width, :] = totals[tile][
                    (i - lo) * width : (i - lo + 1) * width, across * width : (across + 1) * width
                ]
            if start == 0:
                base = len(kept) * width
                packed_ref[base:, :] = jnp.zeros((packed_ref.shape[0] - base, width), F32)
                vec = jnp.concatenate([acc[0:1, :] for acc in acc_refs], 1) + dot_nn(t_ref[0], prior)
                for i in range(count):
                    packed_ref[base + i : base + i + 1, :] = vec[:, i * width : (i + 1) * width]
            half = packed_ref.shape[0] // 2
            upper = place_ref[2 + n]
            out_refs[2 * n][...] = packed_ref[pl.ds(pl.multiple_of(upper * half, SUB), half), :]
            out_refs[2 * n + 1][...] = packed_ref[
                pl.ds(pl.multiple_of((1 - upper) * half, SUB), half), :
            ]


def packed_rows(lo, hi, count, width, sensors):
    return len(upper_blocks(lo, hi, count)) * width + (SUB * sensors if lo == 0 else 0)


def local_gram(spans, place, values, blocks, noise, reading, avail, prior, target, count, sensors):
    rows, pair = values.shape
    width = pair // 2
    lo, hi = spans[0][0], spans[-1][1]
    share = prior.shape[0] // sensors
    totals = [packed_rows(first, past, count, width, sensors) for first, past in spans]
    top = 16 if lo == 0 else 0
    chunk = min(CHUNK, rows)
    line = pl.BlockSpec((1, chunk), lambda c, place: (0, c))
    halves = [total // 2 for total in totals for _ in range(2)]
    return pl.pallas_call(
        functools.partial(gram_kernel, count, spans),
        grid_spec=pltpu.PrefetchScalarGridSpec(
            num_scalar_prefetch=1,
            grid=(rows // chunk,),
            in_specs=[
                pl.BlockSpec((chunk, pair), lambda c, place: (c, 0)),
                pl.BlockSpec((2, chunk), lambda c, place: (0, c)),
                line,
                line,
                line,
                pl.BlockSpec((share, prior.shape[1]), lambda c, place: (place[0], 0)),
                pl.BlockSpec((1, 1, share), lambda c, place: (place[0], 0, 0)),
            ],
            out_specs=[pl.BlockSpec((half, width), lambda c, place: (0, 0)) for half in halves],
            scratch_shapes=[pltpu.VMEM((total, width), F32) for total in totals]
            + [pltpu.VMEM((top + (count - lo) * width, chunk), BF16)]
            + [
                pltpu.VMEM((top + (stop - lo) * width, (end - first) * width), F32)
                for first, end, stop in tiles(lo, hi, count)
            ],
        ),
        out_shape=[jax.ShapeDtypeStruct((half, width), F32) for half in halves],
        compiler_params=pltpu.CompilerParams(vmem_limit_bytes=VMEM_BYTES),
        cost_estimate=pl.CostEstimate(
            flops=2 * rows * width * sum(totals), bytes_accessed=rows * pair * 2, transcendentals=0
        ),
        name="gram",
    )(place, values, blocks, noise, reading, avail, prior, target.reshape(sensors, 1, share))


def frame_kernel(count, spans, f_ref, *out_refs):
    width = out_refs[0].shape[1]
    parts = [f_ref[:, i * width : (i + 1) * width] for i in range(count)]
    for (lo, hi), out_ref in zip(spans, out_refs):
        kept = upper_blocks(lo, hi, count)
        for n, (i, j) in enumerate(kept):
            out_ref[n * width : (n + 1) * width, :] = column_of(parts[i]) * parts[j]
        base = len(kept) * width
        if lo == 0:
            out_ref[base:, :] = jnp.zeros((out_ref.shape[0] - base, width), F32)
            for i in range(count):
                out_ref[base + i : base + i + 1, :] = parts[i]


def frame_scales(inverse, spans, count, width, sensors):
    shapes = [(packed_rows(lo, hi, count, width, sensors), width) for lo, hi in spans]
    size = sum(rows * width for rows, width in shapes)
    return pl.pallas_call(
        functools.partial(frame_kernel, count, spans),
        out_shape=[jax.ShapeDtypeStruct(shape, F32) for shape in shapes],
        cost_estimate=pl.CostEstimate(flops=size, bytes_accessed=size * 4, transcendentals=0),
        name="frames",
    )(inverse)


def spread(x, index, axis):
    return jnp.broadcast_to(lax.slice_in_dim(x, index, index + 1, axis=axis), x.shape)


def split3(x):
    a = x.astype(BF16)
    rest = x - a.astype(F32)
    b = rest.astype(BF16)
    return a, b, (rest - b.astype(F32)).astype(BF16)


def far_product(top, both):
    a, b, c = split3(both)
    left = jnp.concatenate([a, a, b, a, c, b], 0)[:, : top.shape[1]]
    right = jnp.concatenate([a, b, a, c, a, b], 0)
    return lax.dot_general(left, right, (((0,), (0,)), ((), ())), preferred_element_type=F32)


def diag_factor(block):
    size = block.shape[0]
    groups = size // SUB
    lane = lax.broadcasted_iota(jnp.int32, (SUB, size), 1)
    sub = lax.broadcasted_iota(jnp.int32, (SUB, size), 0)
    left = [block[SUB * r : SUB * (r + 1), :] for r in range(groups)]
    right = [(lane == sub + SUB * r).astype(F32) for r in range(groups)]
    tops = []
    lows = []
    for g in range(groups):
        near = min(groups, g + 1 + FAR)
        cols = {r: [spread(left[r], SUB * g + k, 1) for k in range(SUB)] for r in range(g, near)}
        s = [[spread(cols[g][k], i, 0) if i >= k else None for k in range(SUB)] for i in range(SUB)]
        xs = [spread(left[g], k, 0) for k in range(SUB)]
        ys = [spread(right[g], k, 0) for k in range(SUB)]
        inv = []
        for k in range(SUB):
            inv.append(lax.rsqrt(s[k][k]))
            for i in range(k + 1, SUB):
                s[i][k] = s[i][k] * inv[k]
            for j in range(k + 1, SUB):
                for i in range(j, SUB):
                    s[i][j] = s[i][j] - s[i][k] * s[j][k]
            xs[k] = xs[k] * inv[k]
            ys[k] = ys[k] * inv[k]
            for i in range(k + 1, SUB):
                xs[i] = xs[i] - s[i][k] * xs[k]
                ys[i] = ys[i] - s[i][k] * ys[k]
        for r in range(g + 1, near):
            ls = cols[r]
            for k in range(SUB):
                ls[k] = ls[k] * inv[k]
                for j in range(k + 1, SUB):
                    ls[j] = ls[j] - s[j][k] * ls[k]
                left[r] = left[r] - ls[k] * xs[k]
                right[r] = right[r] - ls[k] * ys[k]
        top, low = xs[0], ys[0]
        for k in range(1, SUB):
            top = jnp.where(sub == k, xs[k], top)
            low = jnp.where(sub == k, ys[k], low)
        if near < groups:
            delta = far_product(top, jnp.concatenate([top, low], 1))
            for r in range(near, groups):
                left[r] = left[r] - delta[SUB * r : SUB * (r + 1), :size]
                right[r] = right[r] - delta[SUB * r : SUB * (r + 1), size:]
        tops.append(jnp.where(lane >= sub + SUB * g, top, 0.0))
        lows.append(low)
    return jnp.concatenate(tops, 0), jnp.concatenate(lows, 0)


def run_panels(count, lo, hi, row_of, s_ref, r_ref, t_ref):
    width = t_ref.shape[1]
    start = lo * width

    s_ref[...] = row_of(lo)

    @pl.loop(0, hi - lo)
    def _(k):
        at = pl.multiple_of(k * width, width)
        upper, inverse = diag_factor(s_ref[:, pl.ds(at, width)])
        t_ref[pl.ds(at, width), :] = inverse
        r_ref[pl.ds(at, width), pl.ds(at, width)] = upper
        for kk in range(hi - lo):

            @pl.when(k == kk)
            def _():
                rest = (kk + 1) * width
                r_ref[kk * width : rest, rest:] = dot_nn(t_ref[kk * width : rest, :], s_ref[:, rest:])
                if lo + kk + 1 < hi:
                    s_ref[:, rest:] = row_of(lo + kk + 1) - dot_tn(
                        r_ref[0:rest, rest : rest + width], r_ref[0:rest, rest:]
                    )


def stage_kernel(count, lo, hi, place_ref, own_ref, other_ref, *refs):
    refs = list(refs)
    before = lo > 0
    last = hi == count
    carry_ref = refs.pop(0) if before else None
    if last:
        frame_ref = refs.pop(0)
        earlier = [(refs.pop(0), refs.pop(0)) for _ in range((len(refs) - 6) // 2)]
        rows_ref, est_ref, r_ref, t_ref = refs[:4]
    else:
        r_ref, t_ref, left_ref = refs[:3]
    x_ref, s_ref = refs[-2:]
    width = x_ref.shape[1]
    states = count * width
    kept = upper_blocks(lo, hi, count)
    half = own_ref.shape[0]
    upper = place_ref[1 + CUT_PLACES.index(lo)]
    x_ref[pl.ds(pl.multiple_of(upper * half, SUB), half), :] = own_ref[...]
    x_ref[pl.ds(pl.multiple_of((1 - upper) * half, SUB), half), :] = other_ref[...]

    def taken_before(k):
        return carry_ref[(k - lo) * width : (k - lo + 1) * width, (k - lo) * width :]

    def vec_column(k):
        base = len(kept) * width
        return column_of(x_ref[base + k : base + k + 1, :])

    def row_of(k):
        parts = [x_ref[pl.ds(kept.index((k, j)) * width, width), :] for j in range(k, count)]
        if before:
            parts.append(jnp.zeros((width, width), F32))
            return jnp.concatenate(parts, 1) + taken_before(k)
        return jnp.concatenate(parts + [vec_column(k)], 1)

    run_panels(count, lo, hi, row_of, s_ref, r_ref, t_ref)
    if not last:
        for k in range(hi, count):
            at = (k - lo) * width
            taken = dot_tn(r_ref[:, at : at + width], r_ref[:, at:])
            rows = slice((k - hi) * width, (k - hi + 1) * width)
            if before:
                left_ref[rows, (k - hi) * width :] = taken_before(k) - taken
            else:
                end = states - k * width
                left_ref[rows, (k - hi) * width : states - hi * width] = -taken[:, :end]
                left_ref[rows, states - hi * width :] = vec_column(k) - taken[:, end:]
        return

    owners = []
    groups = []
    for r, t in earlier + [(r_ref, t_ref)]:
        groups.append((r, t, len(owners)))
        owners += [groups[-1]] * (t.shape[0] // width)
    solved = [None] * count
    for k in reversed(range(count)):
        r, t, first = owners[k]
        mine = slice((k - first) * width, (k - first + 1) * width)
        right = r[mine, states - first * width :]
        if k + 1 < count:
            right = right - dot_nn(
                r[mine, (k + 1 - first) * width : states - first * width],
                jnp.concatenate(solved[k + 1 :], 0),
            )
        solved[k] = dot_tn(t[mine, :], right)
    for k in range(count):
        cols = slice(k * width, (k + 1) * width)
        est_ref[:, cols] = solved[k].T[0:1, :] / frame_ref[:, cols]
    share = rows_ref.shape[0]
    mine = place_ref[0] * share
    for r, t, first in groups:
        inside = jnp.logical_and(mine >= first * width, mine < first * width + t.shape[0])

        @pl.when(inside)
        def _(r=r, first=first):
            at = pl.multiple_of(mine - first * width, SUB)
            if first:
                rows_ref[:, : first * width] = jnp.zeros((share, first * width), F32)
            for j in range(first, count):
                cols = slice(j * width, (j + 1) * width)
                row = r[pl.ds(at, share), (j - first) * width : (j - first + 1) * width]
                rows_ref[:, cols] = jnp.where(mine < (j + 1) * width, row * frame_ref[:, cols], 0.0)


def factor_stage(span, place, halves, carry, earlier, frame, count, share):
    lo, hi = span
    width = halves[0].shape[1]
    states = count * width
    rest = states - lo * width
    rows = (hi - lo) * width
    last = hi == count
    vmem = pl.BlockSpec(memory_space=pltpu.VMEM)
    operands = list(halves)
    if lo:
        operands.append(carry)
    parts = [(rows, rest + width), (rows, width)]
    if last:
        operands += [frame] + [x for pair in earlier for x in pair]
        outs = [(share, states), (1, states)]
    else:
        outs = parts + [(states - hi * width, states - hi * width + width)]
    scratch = (parts if last else []) + [(2 * halves[0].shape[0], width), (width, rest + width)]
    return pl.pallas_call(
        functools.partial(stage_kernel, count, lo, hi),
        in_specs=[pl.BlockSpec(memory_space=pltpu.SMEM)] + [vmem] * len(operands),
        out_specs=[vmem] * len(outs),
        out_shape=[jax.ShapeDtypeStruct(shape, F32) for shape in outs],
        scratch_shapes=[pltpu.VMEM(shape, F32) for shape in scratch],
        compiler_params=pltpu.CompilerParams(vmem_limit_bytes=VMEM_BYTES),
        cost_estimate=pl.CostEstimate(
            flops=(hi - lo) * FACTOR_FLOPS, bytes_accessed=8 * halves[0].size, transcendentals=rows
        ),
        name="factor",
    )(place, *operands)


def exchange(x, axis, mask):
    return lax.ppermute(x, axis, [(i, i ^ mask) for i in range(lax.axis_size(axis))])


def after(x, other):
    return lax.optimization_barrier((x, other))[0]


def is_upper(axis, bit):
    return ((lax.axis_index(axis) & bit) != 0).astype(jnp.int32)


def halve(x, axis, bit):
    half = x.shape[0] // 2
    upper = is_upper(axis, bit)
    return (
        lax.dynamic_slice_in_dim(x, upper * half, half, 0),
        lax.dynamic_slice_in_dim(x, (1 - upper) * half, half, 0),
    )


def per_device(values, blocks, noise_scale, readings, available, decay, prior_factor, prior_target):
    states = prior_factor.shape[0]
    width = values.shape[1] // 2
    count = states // width
    sensors = lax.axis_size("sensor")
    steps = lax.axis_size("tm")
    share = states // sensors
    own = lax.axis_index("sensor").astype(jnp.int32)
    time = lax.axis_index("tm")
    bits = [1 << n for n in range(sensors.bit_length() - 1)]
    turned = [bits[1], bits[0]] + bits[2:]
    spans = [(0, CUTS[0]), (CUTS[0], CUTS[1]), (CUTS[1], count)]
    orders = [bits, turned, bits]
    uppers = [is_upper("sensor", order[0]) for order in orders]
    begins = (time == 0).astype(jnp.int32)

    def earlier(x, by):
        return lax.ppermute(x, "tm", [(i, i + by) for i in range(steps - by)])

    rest = (values, blocks.T, noise_scale, readings, available, prior_factor, prior_target)
    halves = list(local_gram(spans[:1], jnp.stack([own, begins, uppers[0]]), *rest, count, sensors))
    place = jnp.stack([own, begins] + uppers[1:])
    place, halves[1] = lax.optimization_barrier((place, halves[1]))
    halves += local_gram(spans[1:], place, *rest, count, sensors)
    decay = after(decay, halves[-1])

    frame = jnp.ones((1, states), F32)
    for by in range(1, steps):
        frame = frame * jnp.where(time >= by, earlier(decay, by), 1.0)
    scales = frame_scales(1.0 / frame, spans, count, width, sensors)

    places = jnp.stack([own] + uppers)
    parts = []

    def stage(step):
        moved = [step(n, part) for n, part in enumerate(parts)]
        for n, (other, combine) in enumerate(moved):
            if n:
                other = after(other, parts[n - 1])
            parts[n] = combine(other)

    def sum_first(n, part):
        return exchange(halves[2 * n + 1], "sensor", orders[n][0]), lambda other: part + other

    def sum_at(level):
        def step(n, part):
            stays, leaves = halve(part, "sensor", orders[n][level])
            return exchange(leaves, "sensor", orders[n][level]), lambda other: stays + other

        return step

    def add_earlier(by):
        return lambda n, part: (earlier(part, by), lambda other: part + other)

    def gather_at(level):
        def step(n, part):
            bit = orders[n][level]

            def combine(other):
                return jnp.where(
                    is_upper("sensor", bit) == 1,
                    jnp.concatenate([other, part], 0),
                    jnp.concatenate([part, other], 0),
                )

            return exchange(part, "sensor", bit), combine

        return step

    parts = halves[0::2]
    stage(sum_first)
    for level in range(1, len(bits)):
        stage(sum_at(level))
    for n, (order, scale) in enumerate(zip(orders, scales)):
        for bit in order:
            scale = halve(scale, "sensor", bit)[0]
        parts[n] = parts[n] * scale
    by = 1
    while by < steps:
        stage(add_earlier(by))
        by *= 2
    for level in reversed(range(1, len(bits))):
        stage(gather_at(level))
    stage(lambda n, part: (exchange(part, "sensor", orders[n][0]), lambda other: (part, other)))
    done = []
    carry = None
    for span, pieces in zip(spans[:-1], parts):
        upper, inverses, carry = factor_stage(span, places, pieces, carry, [], frame, count, share)
        done.append((upper, inverses))
    rows, estimate = factor_stage(spans[-1], places, parts[-1], carry, done, frame, count, share)
    return rows[None], estimate


def solution(mesh):
    placed = (
        P("sensor", None),
        P("sensor", None),
        P("tm", "sensor"),
        P("tm", "sensor"),
        P("tm", "sensor"),
        P("tm", None),
        P(),
        P(),
    )
    return jax.shard_map(
        per_device,
        mesh=mesh,
        in_specs=placed,
        out_specs=(P("tm", "sensor", None), P("tm", None)),
        check_vma=False,
    )
```

```python
import functools

import jax
import jax.numpy as jnp
from jax import lax
from jax.experimental import pallas as pl
from jax.experimental.pallas import tpu as pltpu
from jax.sharding import PartitionSpec as P

HI = lax.Precision.HIGHEST
SUB = 8
CHUNK = 2048
VMEM_BYTES = 60 << 20
CUTS = (2,)
CUT_PLACES = (0,) + CUTS
FAR = 3
TIED = ()
TURNED = (1,)
FACTOR_FLOPS = 5 * 10**9
BF16 = jnp.bfloat16
F32 = jnp.float32


def upper_blocks(lo, hi, count):
    return [(i, j) for i in range(lo, hi) for j in range(i, count)]


def column_of(row):
    n = row.shape[1]
    return jnp.broadcast_to(row, (n, n)).T


def nt(a, b):
    return lax.dot_general(a, b, (((1,), (1,)), ((), ())), preferred_element_type=F32)


def dot_tn(a, b):
    return lax.dot_general(a, b, (((0,), (0,)), ((), ())), precision=HI, preferred_element_type=F32)


def dot_nn(a, b):
    return jnp.dot(a, b, precision=HI, preferred_element_type=F32)


def tiles(lo, hi, count):
    spans = [(j, min(j + 2, count)) for j in range(lo, count, 2)]
    return [(first, end, min(end, hi)) for first, end in spans]


def gram_kernel(
    count, spans, number, place_ref, v_ref, b_ref, n_ref, r_ref, a_ref, p_ref, t_ref, *refs
):
    out_refs = refs[: 2 * len(spans)]
    packed_refs = refs[2 * len(spans) : 3 * len(spans)]
    wide_ref, *acc_refs = refs[3 * len(spans) :]
    lo, hi = spans[0][0], spans[-1][1]
    step = pl.program_id(0)
    width = v_ref.shape[1] // 2
    pair = 2 * width
    chunk = v_ref.shape[0]
    top = 16 if lo == 0 else 0

    @pl.when(step == 0)
    def _():
        for acc in acc_refs:
            acc[...] = jnp.zeros_like(acc)

    factor = a_ref[...].astype(F32) / n_ref[...]
    if top:
        wide_ref[0:top, :] = jnp.broadcast_to(r_ref[...] * factor, (top, chunk)).astype(BF16)
    rows = lax.broadcasted_iota(jnp.int32, (pair, pair), 0)
    cols = lax.broadcasted_iota(jnp.int32, (pair, pair), 1)
    eye = (rows == cols).astype(F32).astype(BF16)
    weighted = (nt(eye, v_ref[...]) * factor).astype(BF16)
    blocks = b_ref[...]
    for b in range(lo, count):
        hit = jnp.where(blocks == b, 1.0, 0.0)
        hit0 = jnp.broadcast_to(hit[0:1], (16, chunk)).astype(BF16)
        hit1 = jnp.broadcast_to(hit[1:2], (16, chunk)).astype(BF16)
        for q in range(0, width, 16):
            at = top + (b - lo) * width + q
            wide_ref[at : at + 16, :] = (
                weighted[q : q + 16] * hit0 + weighted[width + q : width + q + 16] * hit1
            )
    columns = tiles(lo, hi, count)
    for (first, end, stop), acc in zip(columns, acc_refs):
        acc[...] += nt(
            wide_ref[0 : top + (stop - lo) * width, :],
            wide_ref[top + (first - lo) * width : top + (end - lo) * width, :],
        )

    @pl.when(step == pl.num_programs(0) - 1)
    def _():
        prior = p_ref[...] * place_ref[1].astype(F32)
        totals = [
            acc[top:, :]
            + dot_tn(prior[:, lo * width : stop * width], prior[:, first * width : end * width])
            for (first, end, stop), acc in zip(columns, acc_refs)
        ]
        for n, (start, past) in enumerate(spans):
            kept = upper_blocks(start, past, count)
            packed_ref = packed_refs[n]
            for m, (i, j) in enumerate(kept):
                tile = (j - lo) // 2
                across = j - columns[tile][0]
                packed_ref[m * width : (m + 1) * width, :] = totals[tile][
                    (i - lo) * width : (i - lo + 1) * width, across * width : (across + 1) * width
                ]
            if start == 0:
                base = len(kept) * width
                packed_ref[base:, :] = jnp.zeros((packed_ref.shape[0] - base, width), F32)
                vec = jnp.concatenate([acc[0:1, :] for acc in acc_refs], 1) + dot_nn(t_ref[0], prior)
                for i in range(count):
                    packed_ref[base + i : base + i + 1, :] = vec[:, i * width : (i + 1) * width]
            half = packed_ref.shape[0] // 2
            upper = place_ref[2 + number + n]
            out_refs[2 * n][...] = packed_ref[pl.ds(pl.multiple_of(upper * half, SUB), half), :]
            out_refs[2 * n + 1][...] = packed_ref[
                pl.ds(pl.multiple_of((1 - upper) * half, SUB), half), :
            ]


def packed_rows(lo, hi, count, width, sensors):
    return len(upper_blocks(lo, hi, count)) * width + (SUB * sensors if lo == 0 else 0)


def local_gram(spans, number, place, values, blocks, noise, reading, avail, prior, target, count, sensors):
    rows, pair = values.shape
    width = pair // 2
    lo, hi = spans[0][0], spans[-1][1]
    share = prior.shape[0] // sensors
    totals = [packed_rows(first, past, count, width, sensors) for first, past in spans]
    top = 16 if lo == 0 else 0
    chunk = min(CHUNK, rows)
    line = pl.BlockSpec((1, chunk), lambda c, place: (0, c))
    halves = [total // 2 for total in totals for _ in range(2)]
    return pl.pallas_call(
        functools.partial(gram_kernel, count, spans, number),
        grid_spec=pltpu.PrefetchScalarGridSpec(
            num_scalar_prefetch=1,
            grid=(rows // chunk,),
            in_specs=[
                pl.BlockSpec((chunk, pair), lambda c, place: (c, 0)),
                pl.BlockSpec((2, chunk), lambda c, place: (0, c)),
                line,
                line,
                line,
                pl.BlockSpec((share, prior.shape[1]), lambda c, place: (place[0], 0)),
                pl.BlockSpec((1, 1, share), lambda c, place: (place[0], 0, 0)),
            ],
            out_specs=[pl.BlockSpec((half, width), lambda c, place: (0, 0)) for half in halves],
            scratch_shapes=[pltpu.VMEM((total, width), F32) for total in totals]
            + [pltpu.VMEM((top + (count - lo) * width, chunk), BF16)]
            + [
                pltpu.VMEM((top + (stop - lo) * width, (end - first) * width), F32)
                for first, end, stop in tiles(lo, hi, count)
            ],
        ),
        out_shape=[jax.ShapeDtypeStruct((half, width), F32) for half in halves],
        compiler_params=pltpu.CompilerParams(vmem_limit_bytes=VMEM_BYTES),
        cost_estimate=pl.CostEstimate(
            flops=2 * rows * width * sum(totals), bytes_accessed=rows * pair * 2, transcendentals=0
        ),
        name="gram",
    )(place, values, blocks, noise, reading, avail, prior, target.reshape(sensors, 1, share))


def decay_kernel(count, spans, place_ref, f_ref, *refs):
    out_refs, packed_refs = refs[: len(spans)], refs[len(spans) :]
    width = out_refs[0].shape[1]
    parts = [f_ref[:, i * width : (i + 1) * width] for i in range(count)]
    for n, (lo, hi) in enumerate(spans):
        packed_ref, out_ref = packed_refs[n], out_refs[n]
        kept = upper_blocks(lo, hi, count)
        for m, (i, j) in enumerate(kept):
            packed_ref[m * width : (m + 1) * width, :] = column_of(parts[i]) * parts[j]
        base = len(kept) * width
        if lo == 0:
            packed_ref[base:, :] = jnp.zeros((packed_ref.shape[0] - base, width), F32)
            for i in range(count):
                packed_ref[base + i : base + i + 1, :] = parts[i]
        at = pl.multiple_of(place_ref[2 + len(spans) + n], SUB)
        out_ref[...] = packed_ref[pl.ds(at, out_ref.shape[0]), :]


def decay_pieces(place, decay, spans, count, width, sensors):
    totals = [packed_rows(lo, hi, count, width, sensors) for lo, hi in spans]
    vmem = pl.BlockSpec(memory_space=pltpu.VMEM)
    size = sum(totals) * width
    return pl.pallas_call(
        functools.partial(decay_kernel, count, spans),
        in_specs=[pl.BlockSpec(memory_space=pltpu.SMEM), vmem],
        out_specs=[vmem] * len(spans),
        out_shape=[jax.ShapeDtypeStruct((total // sensors, width), F32) for total in totals],
        scratch_shapes=[pltpu.VMEM((total, width), F32) for total in totals],
        cost_estimate=pl.CostEstimate(flops=size, bytes_accessed=size, transcendentals=0),
        compiler_params=pltpu.CompilerParams(vmem_limit_bytes=VMEM_BYTES),
        name="decays",
    )(place, decay)


def spread(x, index, axis):
    return jnp.broadcast_to(lax.slice_in_dim(x, index, index + 1, axis=axis), x.shape)


def split3(x):
    a = x.astype(BF16)
    rest = x - a.astype(F32)
    b = rest.astype(BF16)
    return a, b, (rest - b.astype(F32)).astype(BF16)


def far_product(top, both):
    a, b, c = split3(both)
    left = jnp.concatenate([a, a, b, a, c, b], 0)[:, : top.shape[1]]
    right = jnp.concatenate([a, b, a, c, a, b], 0)
    return lax.dot_general(left, right, (((0,), (0,)), ((), ())), preferred_element_type=F32)


def diag_factor(block):
    size = block.shape[0]
    groups = size // SUB
    lane = lax.broadcasted_iota(jnp.int32, (SUB, size), 1)
    sub = lax.broadcasted_iota(jnp.int32, (SUB, size), 0)
    left = [block[SUB * r : SUB * (r + 1), :] for r in range(groups)]
    right = [(lane == sub + SUB * r).astype(F32) for r in range(groups)]
    tops = []
    lows = []
    for g in range(groups):
        near = min(groups, g + 1 + FAR)
        cols = {r: [spread(left[r], SUB * g + k, 1) for k in range(SUB)] for r in range(g, near)}
        mine, top, low = cols[g], left[g], right[g]
        inv, xs, ys = [], [], []
        below = [[None] * SUB for _ in range(SUB)]
        for k in range(SUB):
            inv.append(spread(lax.rsqrt(mine[k]), k, 0))
            mine[k] = mine[k] * inv[k]
            for i in range(k + 1, SUB):
                below[i][k] = spread(mine[k], i, 0)
                mine[i] = mine[i] - mine[k] * below[i][k]
            xs.append(spread(top, k, 0) * inv[k])
            ys.append(spread(low, k, 0) * inv[k])
            under = jnp.where(sub > k, mine[k], 0.0)
            top = top - under * xs[k]
            low = low - under * ys[k]
        for r in range(g + 1, near):
            ls = cols[r]
            for k in range(SUB):
                ls[k] = ls[k] * inv[k]
                for j in range(k + 1, SUB):
                    ls[j] = ls[j] - below[j][k] * ls[k]
                left[r] = left[r] - ls[k] * xs[k]
                right[r] = right[r] - ls[k] * ys[k]
        scale = inv[0]
        for k in range(1, SUB):
            scale = jnp.where(sub == k, inv[k], scale)
        top, low = top * scale, low * scale
        if near < groups:
            delta = far_product(top, jnp.concatenate([top, low], 1))
            for r in range(near, groups):
                left[r] = left[r] - delta[SUB * r : SUB * (r + 1), :size]
                right[r] = right[r] - delta[SUB * r : SUB * (r + 1), size:]
        tops.append(jnp.where(lane >= sub + SUB * g, top, 0.0))
        lows.append(low)
    return jnp.concatenate(tops, 0), jnp.concatenate(lows, 0)


def run_panels(count, lo, hi, row_of, s_ref, r_ref, t_ref):
    width = t_ref.shape[1]
    start = lo * width

    s_ref[...] = row_of(lo)

    @pl.loop(0, hi - lo)
    def _(k):
        at = pl.multiple_of(k * width, width)
        upper, inverse = diag_factor(s_ref[:, pl.ds(at, width)])
        t_ref[pl.ds(at, width), :] = inverse
        r_ref[pl.ds(at, width), pl.ds(at, width)] = upper
        for kk in range(hi - lo):

            @pl.when(k == kk)
            def _():
                rest = (kk + 1) * width
                r_ref[kk * width : rest, rest:] = dot_nn(t_ref[kk * width : rest, :], s_ref[:, rest:])
                if lo + kk + 1 < hi:
                    s_ref[:, rest:] = row_of(lo + kk + 1) - dot_tn(
                        r_ref[0:rest, rest : rest + width], r_ref[0:rest, rest:]
                    )


def stage_kernel(count, lo, hi, place_ref, own_ref, other_ref, *refs):
    refs = list(refs)
    before = lo > 0
    last = hi == count
    carry_ref = refs.pop(0) if before else None
    if last:
        earlier = [(refs.pop(0), refs.pop(0)) for _ in range((len(refs) - 6) // 2)]
        rows_ref, est_ref, r_ref, t_ref = refs[:4]
    else:
        r_ref, t_ref, left_ref = refs[:3]
    x_ref, s_ref = refs[-2:]
    width = x_ref.shape[1]
    states = count * width
    kept = upper_blocks(lo, hi, count)
    half = own_ref.shape[0]
    upper = place_ref[2 + CUT_PLACES.index(lo)]
    x_ref[pl.ds(pl.multiple_of(upper * half, SUB), half), :] = own_ref[...]
    x_ref[pl.ds(pl.multiple_of((1 - upper) * half, SUB), half), :] = other_ref[...]

    def taken_before(k):
        return carry_ref[(k - lo) * width : (k - lo + 1) * width, (k - lo) * width :]

    def vec_column(k):
        base = len(kept) * width
        return column_of(x_ref[base + k : base + k + 1, :])

    def row_of(k):
        parts = [x_ref[pl.ds(kept.index((k, j)) * width, width), :] for j in range(k, count)]
        if before:
            parts.append(jnp.zeros((width, width), F32))
            return jnp.concatenate(parts, 1) + taken_before(k)
        return jnp.concatenate(parts + [vec_column(k)], 1)

    run_panels(count, lo, hi, row_of, s_ref, r_ref, t_ref)
    if not last:
        for k in range(hi, count):
            at = (k - lo) * width
            taken = dot_tn(r_ref[:, at : at + width], r_ref[:, at:])
            rows = slice((k - hi) * width, (k - hi + 1) * width)
            if before:
                left_ref[rows, (k - hi) * width :] = taken_before(k) - taken
            else:
                end = states - k * width
                left_ref[rows, (k - hi) * width : states - hi * width] = -taken[:, :end]
                left_ref[rows, states - hi * width :] = vec_column(k) - taken[:, end:]
        return

    owners = []
    groups = []
    for r, t in earlier + [(r_ref, t_ref)]:
        groups.append((r, t, len(owners)))
        owners += [groups[-1]] * (t.shape[0] // width)
    taken = [jnp.zeros((width, width), F32)] * count
    for k in reversed(range(count)):
        r, t, first = owners[k]
        mine = slice((k - first) * width, (k - first + 1) * width)
        right = r[mine, states - first * width :] - jnp.sum(taken[k], axis=1, keepdims=True)
        solved = jnp.sum(t[mine, :] * right, axis=0, keepdims=True)
        cols = slice(k * width, (k + 1) * width)
        est_ref[:, cols] = solved
        for i in range(k):
            r, t, first = owners[i]
            rows = slice((i - first) * width, (i - first + 1) * width)
            taken[i] = taken[i] + r[rows, (k - first) * width : (k - first + 1) * width] * solved
    share = rows_ref.shape[0]
    mine = place_ref[0] * share
    for r, t, first in groups:
        inside = jnp.logical_and(mine >= first * width, mine < first * width + t.shape[0])

        @pl.when(inside)
        def _(r=r, first=first):
            at = pl.multiple_of(mine - first * width, SUB)
            if first:
                rows_ref[:, : first * width] = jnp.zeros((share, first * width), F32)
            for j in range(first, count):
                cols = slice(j * width, (j + 1) * width)
                row = r[pl.ds(at, share), (j - first) * width : (j - first + 1) * width]
                rows_ref[:, cols] = jnp.where(mine < (j + 1) * width, row, 0.0)


def factor_stage(span, place, halves, carry, earlier, count, share):
    lo, hi = span
    width = halves[0].shape[1]
    states = count * width
    rest = states - lo * width
    rows = (hi - lo) * width
    last = hi == count
    vmem = pl.BlockSpec(memory_space=pltpu.VMEM)
    operands = list(halves)
    if lo:
        operands.append(carry)
    parts = [(rows, rest + width), (rows, width)]
    if last:
        operands += [x for pair in earlier for x in pair]
        outs = [(share, states), (1, states)]
    else:
        outs = parts + [(states - hi * width, states - hi * width + width)]
    scratch = (parts if last else []) + [(2 * halves[0].shape[0], width), (width, rest + width)]
    return pl.pallas_call(
        functools.partial(stage_kernel, count, lo, hi),
        in_specs=[pl.BlockSpec(memory_space=pltpu.SMEM)] + [vmem] * len(operands),
        out_specs=[vmem] * len(outs),
        out_shape=[jax.ShapeDtypeStruct(shape, F32) for shape in outs],
        scratch_shapes=[pltpu.VMEM(shape, F32) for shape in scratch],
        compiler_params=pltpu.CompilerParams(vmem_limit_bytes=VMEM_BYTES),
        cost_estimate=pl.CostEstimate(
            flops=(hi - lo) * FACTOR_FLOPS, bytes_accessed=8 * halves[0].size, transcendentals=rows
        ),
        name="factor",
    )(place, *operands)


def exchange(x, axis, mask):
    return lax.ppermute(x, axis, [(i, i ^ mask) for i in range(lax.axis_size(axis))])


def after(x, other):
    return lax.optimization_barrier((x, other))[0]


def is_upper(axis, bit):
    return ((lax.axis_index(axis) & bit) != 0).astype(jnp.int32)


def halve(x, axis, bit):
    half = x.shape[0] // 2
    upper = is_upper(axis, bit)
    return (
        lax.dynamic_slice_in_dim(x, upper * half, half, 0),
        lax.dynamic_slice_in_dim(x, (1 - upper) * half, half, 0),
    )


def per_device(values, blocks, noise_scale, readings, available, decay, prior_factor, prior_target):
    states = prior_factor.shape[0]
    width = values.shape[1] // 2
    count = states // width
    sensors = lax.axis_size("sensor")
    steps = lax.axis_size("tm")
    share = states // sensors
    own = lax.axis_index("sensor").astype(jnp.int32)
    time = lax.axis_index("tm")
    bits = [1 << n for n in range(sensors.bit_length() - 1)]
    turned = [bits[1], bits[0]] + bits[2:]
    spans = list(zip((0,) + CUTS, CUTS + (count,)))
    orders = [turned if n in TURNED else bits for n in range(len(spans))]
    uppers = [is_upper("sensor", order[0]) for order in orders]
    begins = (time == 0).astype(jnp.int32)

    def earlier(x, by):
        return lax.ppermute(x, "tm", [(i, i + by) for i in range(steps - by)])

    rest = (values, blocks.T, noise_scale, readings, available, prior_factor, prior_target)
    sizes = [packed_rows(lo, hi, count, width, sensors) for lo, hi in spans]
    offsets = [
        sum(is_upper("sensor", bit) * (size >> (n + 1)) for n, bit in enumerate(order))
        for size, order in zip(sizes, orders)
    ]
    place = jnp.stack([own, begins] + uppers + offsets)
    halves = list(local_gram(spans[:1], 0, place, *rest, count, sensors))
    later, halves[1] = lax.optimization_barrier((place, halves[1]))
    halves += local_gram(spans[1:], 1, later, *rest, count, sensors)
    own_decay = decay_pieces(place, decay, spans, count, width, sensors)
    decay = after(decay, halves[-1])
    shifted = {gap: earlier(decay, gap) for gap in range(1, steps // 2)}

    parts = []

    def stage(step):
        moved = [step(n, part) for n, part in enumerate(parts)]
        for n, (other, combine) in enumerate(moved):
            if n and n in TIED:
                other = after(other, parts[n - 1])
            parts[n] = combine(other)

    def sum_first(n, part):
        return exchange(halves[2 * n + 1], "sensor", orders[n][0]), lambda other: part + other

    def sum_at(level):
        def step(n, part):
            stays, leaves = halve(part, "sensor", orders[n][level])
            return exchange(leaves, "sensor", orders[n][level]), lambda other: stays + other

        return step

    def add_earlier(by):
        between = 1.0
        for gap in range(1, by):
            between = between * shifted[gap]
        decays = decay_pieces(place, between, spans, count, width, sensors) if by > 1 else None

        def step(n, part):
            other = earlier(part * own_decay[n], by)
            if by > 1:
                other = other * decays[n]
            return other, lambda other: part + other

        return step

    def gather_at(level):
        def step(n, part):
            bit = orders[n][level]

            def combine(other):
                return jnp.where(
                    is_upper("sensor", bit) == 1,
                    jnp.concatenate([other, part], 0),
                    jnp.concatenate([part, other], 0),
                )

            return exchange(part, "sensor", bit), combine

        return step

    parts = halves[0::2]
    stage(sum_first)

    stage(sum_at(1))

    for level in range(2, len(bits)):
        stage(sum_at(level))
    by = 1
    while by < steps:
        stage(add_earlier(by))
        by *= 2
    for level in reversed(range(1, len(bits))):
        stage(gather_at(level))
    stage(lambda n, part: (exchange(part, "sensor", orders[n][0]), lambda other: (part, other)))
    done = []
    carry = None
    for span, pieces in zip(spans[:-1], parts):
        upper, inverses, carry = factor_stage(span, place, pieces, carry, [], count, share)
        done.append((upper, inverses))
    rows, estimate = factor_stage(spans[-1], place, parts[-1], carry, done, count, share)
    return rows[None], estimate


def solution(mesh):
    placed = (
        P("sensor", None),
        P("sensor", None),
        P("tm", "sensor"),
        P("tm", "sensor"),
        P("tm", "sensor"),
        P("tm", None),
        P(),
        P(),
    )
    return jax.shard_map(
        per_device,
        mesh=mesh,
        in_specs=placed,
        out_specs=(P("tm", "sensor", None), P("tm", None)),
        check_vma=False,
    )
```

```python
import functools

import jax
import jax.numpy as jnp
from jax import lax
from jax.experimental import pallas as pl
from jax.experimental.pallas import tpu as pltpu
from jax.sharding import PartitionSpec as P

HI = lax.Precision.HIGHEST
SUB = 8
CHUNK = 2048
VMEM_BYTES = 60 << 20
FACTOR_VMEM_BYTES = 24 << 20
CUTS = (2,)
CUT_PLACES = (0,) + CUTS
FAR = 3
TURNED = (1,)
FACTOR_FLOPS = 5 * 10**9
BF16 = jnp.bfloat16
F32 = jnp.float32


def upper_blocks(lo, hi, count):
    return [(i, j) for i in range(lo, hi) for j in range(i, count)]


def column_of(row):
    n = row.shape[1]
    return jnp.broadcast_to(row, (n, n)).T


def nt(a, b):
    return lax.dot_general(a, b, (((1,), (1,)), ((), ())), preferred_element_type=F32)


def split3(x):
    a = x.astype(BF16)
    rest = x - a.astype(F32)
    b = rest.astype(BF16)
    return a, b, (rest - b.astype(F32)).astype(BF16)


def exact_dot(left, right, axis):
    a, b, c = split3(left)
    left = jnp.concatenate([a, a, b, a, c, b], axis)
    a, b, c = split3(right)
    right = jnp.concatenate([a, b, a, c, a, b], 0)
    return lax.dot_general(left, right, (((axis,), (0,)), ((), ())), preferred_element_type=F32)


def dot_tn(a, b):
    return exact_dot(a, b, 0)


def dot_nn(a, b):
    return exact_dot(a, b, 1)


def tiles(lo, hi, count):
    spans = [(j, min(j + 2, count)) for j in range(lo, count, 2)]
    return [(first, end, min(end, hi)) for first, end in spans]


def gram_kernel(
    count, spans, number, place_ref, v_ref, b_ref, n_ref, r_ref, a_ref, p_ref, t_ref, *refs
):
    out_refs = refs[: 2 * len(spans)]
    packed_refs = refs[2 * len(spans) : 3 * len(spans)]
    wide_ref, *acc_refs = refs[3 * len(spans) :]
    lo, hi = spans[0][0], spans[-1][1]
    step = pl.program_id(0)
    width = v_ref.shape[1] // 2
    pair = 2 * width
    chunk = v_ref.shape[0]
    top = 16 if lo == 0 else 0

    @pl.when(step == 0)
    def _():
        for acc in acc_refs:
            acc[...] = jnp.zeros_like(acc)

    factor = a_ref[...].astype(F32) / n_ref[...]
    if top:
        wide_ref[0:top, :] = jnp.broadcast_to(r_ref[...] * factor, (top, chunk)).astype(BF16)
    rows = lax.broadcasted_iota(jnp.int32, (pair, pair), 0)
    cols = lax.broadcasted_iota(jnp.int32, (pair, pair), 1)
    eye = (rows == cols).astype(F32).astype(BF16)
    weighted = (nt(eye, v_ref[...]) * factor).astype(BF16)
    blocks = b_ref[...]
    for b in range(lo, count):
        hit = jnp.where(blocks == b, 1.0, 0.0)
        hit0 = jnp.broadcast_to(hit[0:1], (16, chunk)).astype(BF16)
        hit1 = jnp.broadcast_to(hit[1:2], (16, chunk)).astype(BF16)
        for q in range(0, width, 16):
            at = top + (b - lo) * width + q
            wide_ref[at : at + 16, :] = (
                weighted[q : q + 16] * hit0 + weighted[width + q : width + q + 16] * hit1
            )
    columns = tiles(lo, hi, count)
    for (first, end, stop), acc in zip(columns, acc_refs):
        acc[...] += nt(
            wide_ref[0 : top + (stop - lo) * width, :],
            wide_ref[top + (first - lo) * width : top + (end - lo) * width, :],
        )

    @pl.when(step == pl.num_programs(0) - 1)
    def _():
        prior = p_ref[...] * place_ref[1].astype(F32)
        totals = [
            acc[top:, :]
            + dot_tn(prior[:, lo * width : stop * width], prior[:, first * width : end * width])
            for (first, end, stop), acc in zip(columns, acc_refs)
        ]
        for n, (start, past) in enumerate(spans):
            kept = upper_blocks(start, past, count)
            packed_ref = packed_refs[n]
            for m, (i, j) in enumerate(kept):
                tile = (j - lo) // 2
                across = j - columns[tile][0]
                packed_ref[m * width : (m + 1) * width, :] = totals[tile][
                    (i - lo) * width : (i - lo + 1) * width, across * width : (across + 1) * width
                ]
            if start == 0:
                base = len(kept) * width
                packed_ref[base:, :] = jnp.zeros((packed_ref.shape[0] - base, width), F32)
                vec = jnp.concatenate([acc[0:1, :] for acc in acc_refs], 1) + jnp.dot(
                    t_ref[0], prior, precision=HI, preferred_element_type=F32
                )
                for i in range(count):
                    packed_ref[base + i : base + i + 1, :] = vec[:, i * width : (i + 1) * width]
            half = packed_ref.shape[0] // 2
            upper = place_ref[2 + number + n]
            out_refs[2 * n][...] = packed_ref[pl.ds(pl.multiple_of(upper * half, SUB), half), :]
            out_refs[2 * n + 1][...] = packed_ref[
                pl.ds(pl.multiple_of((1 - upper) * half, SUB), half), :
            ]


def packed_rows(lo, hi, count, width, sensors):
    return len(upper_blocks(lo, hi, count)) * width + (SUB * sensors if lo == 0 else 0)


def local_gram(spans, number, place, values, blocks, noise, reading, avail, prior, target, count, sensors):
    rows, pair = values.shape
    width = pair // 2
    lo, hi = spans[0][0], spans[-1][1]
    share = prior.shape[0] // sensors
    totals = [packed_rows(first, past, count, width, sensors) for first, past in spans]
    top = 16 if lo == 0 else 0
    chunk = min(CHUNK, rows)
    line = pl.BlockSpec((1, chunk), lambda c, place: (0, c))
    halves = [total // 2 for total in totals for _ in range(2)]
    return pl.pallas_call(
        functools.partial(gram_kernel, count, spans, number),
        grid_spec=pltpu.PrefetchScalarGridSpec(
            num_scalar_prefetch=1,
            grid=(rows // chunk,),
            in_specs=[
                pl.BlockSpec((chunk, pair), lambda c, place: (c, 0)),
                pl.BlockSpec((2, chunk), lambda c, place: (0, c)),
                line,
                line,
                line,
                pl.BlockSpec((share, prior.shape[1]), lambda c, place: (place[0], 0)),
                pl.BlockSpec((1, 1, share), lambda c, place: (place[0], 0, 0)),
            ],
            out_specs=[pl.BlockSpec((half, width), lambda c, place: (0, 0)) for half in halves],
            scratch_shapes=[pltpu.VMEM((total, width), F32) for total in totals]
            + [pltpu.VMEM((top + (count - lo) * width, chunk), BF16)]
            + [
                pltpu.VMEM((top + (stop - lo) * width, (end - first) * width), F32)
                for first, end, stop in tiles(lo, hi, count)
            ],
        ),
        out_shape=[jax.ShapeDtypeStruct((half, width), F32) for half in halves],
        compiler_params=pltpu.CompilerParams(vmem_limit_bytes=VMEM_BYTES),
        cost_estimate=pl.CostEstimate(
            flops=2 * rows * width * sum(totals), bytes_accessed=rows * pair * 2, transcendentals=0
        ),
        name="gram",
    )(place, values, blocks, noise, reading, avail, prior, target.reshape(sensors, 1, share))


def decay_kernel(count, spans, place_ref, f_ref, *refs):
    out_refs, packed_refs = refs[: len(spans)], refs[len(spans) :]
    width = out_refs[0].shape[1]
    parts = [f_ref[:, i * width : (i + 1) * width] for i in range(count)]
    for n, (lo, hi) in enumerate(spans):
        packed_ref, out_ref = packed_refs[n], out_refs[n]
        kept = upper_blocks(lo, hi, count)
        for m, (i, j) in enumerate(kept):
            packed_ref[m * width : (m + 1) * width, :] = column_of(parts[i]) * parts[j]
        base = len(kept) * width
        if lo == 0:
            packed_ref[base:, :] = jnp.zeros((packed_ref.shape[0] - base, width), F32)
            for i in range(count):
                packed_ref[base + i : base + i + 1, :] = parts[i]
        at = pl.multiple_of(place_ref[2 + len(spans) + n], SUB)
        out_ref[...] = packed_ref[pl.ds(at, out_ref.shape[0]), :]


def decay_pieces(place, decay, spans, count, width, sensors):
    totals = [packed_rows(lo, hi, count, width, sensors) for lo, hi in spans]
    vmem = pl.BlockSpec(memory_space=pltpu.VMEM)
    size = sum(totals) * width
    return pl.pallas_call(
        functools.partial(decay_kernel, count, spans),
        in_specs=[pl.BlockSpec(memory_space=pltpu.SMEM), vmem],
        out_specs=[vmem] * len(spans),
        out_shape=[jax.ShapeDtypeStruct((total // sensors, width), F32) for total in totals],
        scratch_shapes=[pltpu.VMEM((total, width), F32) for total in totals],
        cost_estimate=pl.CostEstimate(flops=size, bytes_accessed=size, transcendentals=0),
        compiler_params=pltpu.CompilerParams(vmem_limit_bytes=VMEM_BYTES),
        name="decays",
    )(place, decay)


def spread(x, index, axis):
    return jnp.broadcast_to(lax.slice_in_dim(x, index, index + 1, axis=axis), x.shape)


def far_product(top, both):
    a, b, c = split3(both)
    left = jnp.concatenate([a, a, b, a, c, b], 0)[:, : top.shape[1]]
    right = jnp.concatenate([a, b, a, c, a, b], 0)
    return lax.dot_general(left, right, (((0,), (0,)), ((), ())), preferred_element_type=F32)


def diag_factor(block):
    size = block.shape[0]
    groups = size // SUB
    lane = lax.broadcasted_iota(jnp.int32, (SUB, size), 1)
    sub = lax.broadcasted_iota(jnp.int32, (SUB, size), 0)
    left = [block[SUB * r : SUB * (r + 1), :] for r in range(groups)]
    right = [(lane == sub + SUB * r).astype(F32) for r in range(groups)]
    tops = []
    lows = []
    for g in range(groups):
        near = min(groups, g + 1 + FAR)
        cols = {r: [spread(left[r], SUB * g + k, 1) for k in range(SUB)] for r in range(g, near)}
        mine, top, low = cols[g], left[g], right[g]
        inv, xs, ys = [], [], []
        below = [[None] * SUB for _ in range(SUB)]
        for k in range(SUB):
            inv.append(spread(lax.rsqrt(mine[k]), k, 0))
            mine[k] = mine[k] * inv[k]
            for i in range(k + 1, SUB):
                below[i][k] = spread(mine[k], i, 0)
                mine[i] = mine[i] - mine[k] * below[i][k]
            xs.append(spread(top, k, 0) * inv[k])
            ys.append(spread(low, k, 0) * inv[k])
            under = jnp.where(sub > k, mine[k], 0.0)
            top = top - under * xs[k]
            low = low - under * ys[k]
        for r in range(g + 1, near):
            ls = cols[r]
            for k in range(SUB):
                ls[k] = ls[k] * inv[k]
                for j in range(k + 1, SUB):
                    ls[j] = ls[j] - below[j][k] * ls[k]
                left[r] = left[r] - ls[k] * xs[k]
                right[r] = right[r] - ls[k] * ys[k]
        scale = inv[0]
        for k in range(1, SUB):
            scale = jnp.where(sub == k, inv[k], scale)
        top, low = top * scale, low * scale
        if near < groups:
            delta = far_product(top, jnp.concatenate([top, low], 1))
            for r in range(near, groups):
                left[r] = left[r] - delta[SUB * r : SUB * (r + 1), :size]
                right[r] = right[r] - delta[SUB * r : SUB * (r + 1), size:]
        tops.append(jnp.where(lane >= sub + SUB * g, top, 0.0))
        lows.append(low)
    return jnp.concatenate(tops, 0), jnp.concatenate(lows, 0)


def run_panels(lo, hi, row_of, r_ref, t_ref):
    width = t_ref.shape[1]
    start = lo * width

    row = row_of(lo)
    for k in range(hi - lo):
        at, end = k * width, (k + 1) * width
        upper, inverse = diag_factor(row[:, :width])
        t_ref[at:end, :] = inverse
        r_ref[at:end, at:end] = upper
        if lo + k + 1 < hi:
            near = dot_nn(inverse, row[:, width : 2 * width])
            r_ref[at:end, end : end + width] = near
            following = row_of(lo + k + 1)
            if k:
                following = following - dot_tn(r_ref[0:at, end : end + width], r_ref[0:at, end:])
            block = following[:, :width] - dot_tn(near, near)
            far = dot_nn(inverse, row[:, 2 * width :])
            r_ref[at:end, end + width :] = far
            row = jnp.concatenate([block, following[:, width:] - dot_tn(near, far)], 1)
        else:
            r_ref[at:end, end:] = dot_nn(inverse, row[:, width:])


def stage_kernel(count, lo, hi, place_ref, own_ref, other_ref, *refs):
    refs = list(refs)
    before = lo > 0
    last = hi == count
    carry_ref = refs.pop(0) if before else None
    if last:
        earlier = [(refs.pop(0), refs.pop(0)) for _ in range((len(refs) - 5) // 2)]
        rows_ref, est_ref, r_ref, t_ref = refs[:4]
    else:
        r_ref, t_ref, left_ref = refs[:3]
    x_ref = refs[-1]
    width = x_ref.shape[1]
    states = count * width
    kept = upper_blocks(lo, hi, count)
    half = own_ref.shape[0]
    upper = place_ref[2 + CUT_PLACES.index(lo)]
    x_ref[pl.ds(pl.multiple_of(upper * half, SUB), half), :] = own_ref[...]
    x_ref[pl.ds(pl.multiple_of((1 - upper) * half, SUB), half), :] = other_ref[...]

    def taken_before(k):
        return carry_ref[(k - lo) * width : (k - lo + 1) * width, (k - lo) * width :]

    def vec_column(k):
        base = len(kept) * width
        return column_of(x_ref[base + k : base + k + 1, :])

    def row_of(k):
        parts = [x_ref[pl.ds(kept.index((k, j)) * width, width), :] for j in range(k, count)]
        if before:
            parts.append(jnp.zeros((width, width), F32))
            return jnp.concatenate(parts, 1) + taken_before(k)
        return jnp.concatenate(parts + [vec_column(k)], 1)

    run_panels(lo, hi, row_of, r_ref, t_ref)
    if not last:
        for k in range(hi, count):
            at = (k - lo) * width
            taken = dot_tn(r_ref[:, at : at + width], r_ref[:, at:])
            rows = slice((k - hi) * width, (k - hi + 1) * width)
            if before:
                left_ref[rows, (k - hi) * width :] = taken_before(k) - taken
            else:
                end = states - k * width
                left_ref[rows, (k - hi) * width : states - hi * width] = -taken[:, :end]
                left_ref[rows, states - hi * width :] = vec_column(k) - taken[:, end:]
        return

    owners = []
    groups = []
    for r, t in earlier + [(r_ref, t_ref)]:
        groups.append((r, t, len(owners)))
        owners += [groups[-1]] * (t.shape[0] // width)
    taken = [jnp.zeros((width, width), F32)] * count
    for k in reversed(range(count)):
        r, t, first = owners[k]
        mine = slice((k - first) * width, (k - first + 1) * width)
        right = r[mine, states - first * width :] - jnp.sum(taken[k], axis=1, keepdims=True)
        solved = jnp.sum(t[mine, :] * right, axis=0, keepdims=True)
        cols = slice(k * width, (k + 1) * width)
        est_ref[:, cols] = solved
        for i in range(k):
            r, t, first = owners[i]
            rows = slice((i - first) * width, (i - first + 1) * width)
            taken[i] = taken[i] + r[rows, (k - first) * width : (k - first + 1) * width] * solved
    share = rows_ref.shape[0]
    mine = place_ref[0] * share
    for r, t, first in groups:
        inside = jnp.logical_and(mine >= first * width, mine < first * width + t.shape[0])

        @pl.when(inside)
        def _(r=r, first=first):
            at = pl.multiple_of(mine - first * width, SUB)
            if first:
                rows_ref[:, : first * width] = jnp.zeros((share, first * width), F32)
            for j in range(first, count):
                cols = slice(j * width, (j + 1) * width)
                row = r[pl.ds(at, share), (j - first) * width : (j - first + 1) * width]
                rows_ref[:, cols] = jnp.where(mine < (j + 1) * width, row, 0.0)


def factor_stage(span, place, halves, carry, earlier, count, share):
    lo, hi = span
    width = halves[0].shape[1]
    states = count * width
    rest = states - lo * width
    rows = (hi - lo) * width
    last = hi == count
    vmem = pl.BlockSpec(memory_space=pltpu.VMEM)
    operands = list(halves)
    if lo:
        operands.append(carry)
    parts = [(rows, rest + width), (rows, width)]
    if last:
        operands += [x for pair in earlier for x in pair]
        outs = [(share, states), (1, states)]
    else:
        outs = parts + [(states - hi * width, states - hi * width + width)]
    scratch = (parts if last else []) + [(2 * halves[0].shape[0], width)]
    return pl.pallas_call(
        functools.partial(stage_kernel, count, lo, hi),
        in_specs=[pl.BlockSpec(memory_space=pltpu.SMEM)] + [vmem] * len(operands),
        out_specs=[vmem] * len(outs),
        out_shape=[jax.ShapeDtypeStruct(shape, F32) for shape in outs],
        scratch_shapes=[pltpu.VMEM(shape, F32) for shape in scratch],
        compiler_params=pltpu.CompilerParams(vmem_limit_bytes=FACTOR_VMEM_BYTES),
        cost_estimate=pl.CostEstimate(
            flops=(hi - lo) * FACTOR_FLOPS, bytes_accessed=8 * halves[0].size, transcendentals=rows
        ),
        name="factor",
    )(place, *operands)


def exchange(x, axis, mask):
    return lax.ppermute(x, axis, [(i, i ^ mask) for i in range(lax.axis_size(axis))])


def after(x, other):
    return lax.optimization_barrier((x, other))[0]


def is_upper(axis, bit):
    return ((lax.axis_index(axis) & bit) != 0).astype(jnp.int32)


def halve(x, axis, bit):
    half = x.shape[0] // 2
    upper = is_upper(axis, bit)
    return (
        lax.dynamic_slice_in_dim(x, upper * half, half, 0),
        lax.dynamic_slice_in_dim(x, (1 - upper) * half, half, 0),
    )


def per_device(values, blocks, noise_scale, readings, available, decay, prior_factor, prior_target):
    states = prior_factor.shape[0]
    width = values.shape[1] // 2
    count = states // width
    sensors = lax.axis_size("sensor")
    steps = lax.axis_size("tm")
    share = states // sensors
    own = lax.axis_index("sensor").astype(jnp.int32)
    time = lax.axis_index("tm")
    bits = [1 << n for n in range(sensors.bit_length() - 1)]
    turned = [bits[1], bits[0]] + bits[2:]
    spans = list(zip((0,) + CUTS, CUTS + (count,)))
    orders = [turned if n in TURNED else bits for n in range(len(spans))]
    uppers = [is_upper("sensor", order[0]) for order in orders]
    begins = (time == 0).astype(jnp.int32)

    def earlier(x, by):
        return lax.ppermute(x, "tm", [(i, i + by) for i in range(steps - by)])

    rest = (values, blocks.T, noise_scale, readings, available, prior_factor, prior_target)
    sizes = [packed_rows(lo, hi, count, width, sensors) for lo, hi in spans]
    offsets = [
        sum(is_upper("sensor", bit) * (size >> (n + 1)) for n, bit in enumerate(order))
        for size, order in zip(sizes, orders)
    ]
    place = jnp.stack([own, begins] + uppers + offsets)
    halves = list(local_gram(spans[:1], 0, place, *rest, count, sensors))
    later, halves[1] = lax.optimization_barrier((place, halves[1]))
    halves += local_gram(spans[1:], 1, later, *rest, count, sensors)
    own_decay = decay_pieces(place, decay, spans, count, width, sensors)
    decay = after(decay, halves[-1])
    shifted = {gap: earlier(decay, gap) for gap in range(1, steps // 2)}

    parts = []

    def stage(step):
        moved = [step(n, part) for n, part in enumerate(parts)]
        for n, (other, combine) in enumerate(moved):
            parts[n] = combine(other)

    def sum_first(n, part):
        return exchange(halves[2 * n + 1], "sensor", orders[n][0]), lambda other: part + other

    def sum_at(level):
        def step(n, part):
            stays, leaves = halve(part, "sensor", orders[n][level])
            return exchange(leaves, "sensor", orders[n][level]), lambda other: stays + other

        return step

    def add_earlier(by):
        between = 1.0
        for gap in range(1, by):
            between = between * shifted[gap]
        decays = decay_pieces(place, between, spans, count, width, sensors) if by > 1 else None

        def step(n, part):
            other = earlier(part * own_decay[n], by)
            if by > 1:
                other = other * decays[n]
            return other, lambda other: part + other

        return step

    def gather_at(level):
        def step(n, part):
            bit = orders[n][level]

            def combine(other):
                return jnp.where(
                    is_upper("sensor", bit) == 1,
                    jnp.concatenate([other, part], 0),
                    jnp.concatenate([part, other], 0),
                )

            return exchange(part, "sensor", bit), combine

        return step

    parts = halves[0::2]
    stage(sum_first)

    stage(sum_at(1))

    for level in range(2, len(bits)):
        stage(sum_at(level))
    by = 1
    while by < steps:
        stage(add_earlier(by))
        by *= 2
    for level in reversed(range(1, len(bits))):
        stage(gather_at(level))
    stage(lambda n, part: (exchange(part, "sensor", orders[n][0]), lambda other: (part, other)))
    done = []
    carry = None
    for span, pieces in zip(spans[:-1], parts):
        upper, inverses, carry = factor_stage(span, place, pieces, carry, [], count, share)
        done.append((upper, inverses))
    rows, estimate = factor_stage(spans[-1], place, parts[-1], carry, done, count, share)
    return rows[None], estimate


def solution(mesh):
    placed = (
        P("sensor", None),
        P("sensor", None),
        P("tm", "sensor"),
        P("tm", "sensor"),
        P("tm", "sensor"),
        P("tm", None),
        P(),
        P(),
    )
    return jax.shard_map(
        per_device,
        mesh=mesh,
        in_specs=placed,
        out_specs=(P("tm", "sensor", None), P("tm", None)),
        check_vma=False,
    )
```

```python
import functools

import jax
import jax.numpy as jnp
from jax import lax
from jax.experimental import pallas as pl
from jax.experimental.pallas import tpu as pltpu
from jax.sharding import PartitionSpec as P

HI = lax.Precision.HIGHEST
SUB = 8
CHUNK = 2048
VMEM_BYTES = 60 << 20
FACTOR_VMEM_BYTES = 24 << 20
CUTS = (2,)
CUT_PLACES = (0,) + CUTS
FAR = 3
TURNED = (1,)
FACTOR_FLOPS = 5 * 10**9
BF16 = jnp.bfloat16
F32 = jnp.float32


def upper_blocks(lo, hi, count):
    return [(i, j) for i in range(lo, hi) for j in range(i, count)]


def column_of(row):
    n = row.shape[1]
    return jnp.broadcast_to(row, (n, n)).T


def nt(a, b):
    return lax.dot_general(a, b, (((1,), (1,)), ((), ())), preferred_element_type=F32)


def split3(x):
    a = x.astype(BF16)
    rest = x - a.astype(F32)
    b = rest.astype(BF16)
    return a, b, (rest - b.astype(F32)).astype(BF16)


def exact_dot(left, right, axis):
    a, b, c = split3(left)
    left = jnp.concatenate([a, a, b, a, c, b], axis)
    a, b, c = split3(right)
    right = jnp.concatenate([a, b, a, c, a, b], 0)
    return lax.dot_general(left, right, (((axis,), (0,)), ((), ())), preferred_element_type=F32)


def dot_tn(a, b):
    return exact_dot(a, b, 0)


def dot_nn(a, b):
    return exact_dot(a, b, 1)


def tiles(lo, hi, count):
    spans = [(j, min(j + 2, count)) for j in range(lo, count, 2)]
    return [(first, end, min(end, hi)) for first, end in spans]


def gram_kernel(
    count, spans, number, place_ref, v_ref, b_ref, n_ref, r_ref, a_ref, p_ref, t_ref, *refs
):
    out_refs = refs[: 2 * len(spans)]
    packed_refs = refs[2 * len(spans) : 3 * len(spans)]
    wide_ref, *acc_refs = refs[3 * len(spans) :]
    lo, hi = spans[0][0], spans[-1][1]
    step = pl.program_id(0)
    width = v_ref.shape[1] // 2
    pair = 2 * width
    chunk = v_ref.shape[0]
    top = 16 if lo == 0 else 0

    @pl.when(step == 0)
    def _():
        for acc in acc_refs:
            acc[...] = jnp.zeros_like(acc)

    factor = a_ref[...].astype(F32) / n_ref[...]
    if top:
        wide_ref[0:top, :] = jnp.broadcast_to(r_ref[...] * factor, (top, chunk)).astype(BF16)
    rows = lax.broadcasted_iota(jnp.int32, (pair, pair), 0)
    cols = lax.broadcasted_iota(jnp.int32, (pair, pair), 1)
    eye = (rows == cols).astype(F32).astype(BF16)
    weighted = (nt(eye, v_ref[...]) * factor).astype(BF16)
    blocks = b_ref[...]
    for b in range(lo, count):
        hit = jnp.where(blocks == b, 1.0, 0.0)
        hit0 = jnp.broadcast_to(hit[0:1], (16, chunk)).astype(BF16)
        hit1 = jnp.broadcast_to(hit[1:2], (16, chunk)).astype(BF16)
        for q in range(0, width, 16):
            at = top + (b - lo) * width + q
            wide_ref[at : at + 16, :] = (
                weighted[q : q + 16] * hit0 + weighted[width + q : width + q + 16] * hit1
            )
    columns = tiles(lo, hi, count)
    for (first, end, stop), acc in zip(columns, acc_refs):
        acc[...] += nt(
            wide_ref[0 : top + (stop - lo) * width, :],
            wide_ref[top + (first - lo) * width : top + (end - lo) * width, :],
        )

    @pl.when(step == pl.num_programs(0) - 1)
    def _():
        prior = p_ref[...] * place_ref[1].astype(F32)
        totals = [
            acc[top:, :]
            + dot_tn(prior[:, lo * width : stop * width], prior[:, first * width : end * width])
            for (first, end, stop), acc in zip(columns, acc_refs)
        ]
        for n, (start, past) in enumerate(spans):
            kept = upper_blocks(start, past, count)
            packed_ref = packed_refs[n]
            for m, (i, j) in enumerate(kept):
                tile = (j - lo) // 2
                across = j - columns[tile][0]
                packed_ref[m * width : (m + 1) * width, :] = totals[tile][
                    (i - lo) * width : (i - lo + 1) * width, across * width : (across + 1) * width
                ]
            if start == 0:
                base = len(kept) * width
                packed_ref[base:, :] = jnp.zeros((packed_ref.shape[0] - base, width), F32)
                vec = jnp.concatenate([acc[0:1, :] for acc in acc_refs], 1) + jnp.dot(
                    t_ref[0], prior, precision=HI, preferred_element_type=F32
                )
                for i in range(count):
                    packed_ref[base + i : base + i + 1, :] = vec[:, i * width : (i + 1) * width]
            half = packed_ref.shape[0] // 2
            upper = place_ref[2 + number + n]
            out_refs[2 * n][...] = packed_ref[pl.ds(pl.multiple_of(upper * half, SUB), half), :]
            out_refs[2 * n + 1][...] = packed_ref[
                pl.ds(pl.multiple_of((1 - upper) * half, SUB), half), :
            ]


def packed_rows(lo, hi, count, width, sensors):
    return len(upper_blocks(lo, hi, count)) * width + (SUB * sensors if lo == 0 else 0)


def local_gram(spans, number, place, values, blocks, noise, reading, avail, prior, target, count, sensors):
    rows, pair = values.shape
    width = pair // 2
    lo, hi = spans[0][0], spans[-1][1]
    share = prior.shape[0] // sensors
    totals = [packed_rows(first, past, count, width, sensors) for first, past in spans]
    top = 16 if lo == 0 else 0
    chunk = min(CHUNK, rows)
    line = pl.BlockSpec((1, chunk), lambda c, place: (0, c))
    halves = [total // 2 for total in totals for _ in range(2)]
    return pl.pallas_call(
        functools.partial(gram_kernel, count, spans, number),
        grid_spec=pltpu.PrefetchScalarGridSpec(
            num_scalar_prefetch=1,
            grid=(rows // chunk,),
            in_specs=[
                pl.BlockSpec((chunk, pair), lambda c, place: (c, 0)),
                pl.BlockSpec((2, chunk), lambda c, place: (0, c)),
                line,
                line,
                line,
                pl.BlockSpec((share, prior.shape[1]), lambda c, place: (place[0], 0)),
                pl.BlockSpec((1, 1, share), lambda c, place: (place[0], 0, 0)),
            ],
            out_specs=[pl.BlockSpec((half, width), lambda c, place: (0, 0)) for half in halves],
            scratch_shapes=[pltpu.VMEM((total, width), F32) for total in totals]
            + [pltpu.VMEM((top + (count - lo) * width, chunk), BF16)]
            + [
                pltpu.VMEM((top + (stop - lo) * width, (end - first) * width), F32)
                for first, end, stop in tiles(lo, hi, count)
            ],
        ),
        out_shape=[jax.ShapeDtypeStruct((half, width), F32) for half in halves],
        compiler_params=pltpu.CompilerParams(vmem_limit_bytes=VMEM_BYTES),
        cost_estimate=pl.CostEstimate(
            flops=2 * rows * width * sum(totals), bytes_accessed=rows * pair * 2, transcendentals=0
        ),
        name="gram",
    )(place, values, blocks, noise, reading, avail, prior, target.reshape(sensors, 1, share))


def decay_kernel(count, spans, place_ref, f_ref, *refs):
    out_refs, packed_refs = refs[: len(spans)], refs[len(spans) :]
    width = out_refs[0].shape[1]
    parts = [f_ref[:, i * width : (i + 1) * width] for i in range(count)]
    for n, (lo, hi) in enumerate(spans):
        packed_ref, out_ref = packed_refs[n], out_refs[n]
        kept = upper_blocks(lo, hi, count)
        for m, (i, j) in enumerate(kept):
            packed_ref[m * width : (m + 1) * width, :] = column_of(parts[i]) * parts[j]
        base = len(kept) * width
        if lo == 0:
            packed_ref[base:, :] = jnp.zeros((packed_ref.shape[0] - base, width), F32)
            for i in range(count):
                packed_ref[base + i : base + i + 1, :] = parts[i]
        at = pl.multiple_of(place_ref[2 + len(spans) + n], SUB)
        out_ref[...] = packed_ref[pl.ds(at, out_ref.shape[0]), :]


def decay_pieces(place, decay, spans, count, width, sensors):
    totals = [packed_rows(lo, hi, count, width, sensors) for lo, hi in spans]
    vmem = pl.BlockSpec(memory_space=pltpu.VMEM)
    size = sum(totals) * width
    return pl.pallas_call(
        functools.partial(decay_kernel, count, spans),
        in_specs=[pl.BlockSpec(memory_space=pltpu.SMEM), vmem],
        out_specs=[vmem] * len(spans),
        out_shape=[jax.ShapeDtypeStruct((total // sensors, width), F32) for total in totals],
        scratch_shapes=[pltpu.VMEM((total, width), F32) for total in totals],
        cost_estimate=pl.CostEstimate(flops=size, bytes_accessed=size, transcendentals=0),
        compiler_params=pltpu.CompilerParams(vmem_limit_bytes=VMEM_BYTES),
        name="decays",
    )(place, decay)


def spread(x, index, axis):
    return jnp.broadcast_to(lax.slice_in_dim(x, index, index + 1, axis=axis), x.shape)


def far_product(top, both):
    a, b, c = split3(both)
    left = jnp.concatenate([a, a, b, a, c, b], 0)[:, : top.shape[1]]
    right = jnp.concatenate([a, b, a, c, a, b], 0)
    return lax.dot_general(left, right, (((0,), (0,)), ((), ())), preferred_element_type=F32)


def diag_factor(block):
    size = block.shape[0]
    groups = size // SUB
    lane = lax.broadcasted_iota(jnp.int32, (SUB, size), 1)
    sub = lax.broadcasted_iota(jnp.int32, (SUB, size), 0)
    left = [block[SUB * r : SUB * (r + 1), :] for r in range(groups)]
    right = [(lane == sub + SUB * r).astype(F32) for r in range(groups)]
    tops = []
    lows = []
    for g in range(groups):
        near = min(groups, g + 1 + FAR)
        cols = {r: [spread(left[r], SUB * g + k, 1) for k in range(SUB)] for r in range(g, near)}
        mine, top, low = cols[g], left[g], right[g]
        inv, xs, ys = [], [], []
        below = [[None] * SUB for _ in range(SUB)]
        for k in range(SUB):
            inv.append(spread(lax.rsqrt(mine[k]), k, 0))
            mine[k] = mine[k] * inv[k]
            for i in range(k + 1, SUB):
                below[i][k] = spread(mine[k], i, 0)
                mine[i] = mine[i] - mine[k] * below[i][k]
            xs.append(spread(top, k, 0) * inv[k])
            ys.append(spread(low, k, 0) * inv[k])
            under = jnp.where(sub > k, mine[k], 0.0)
            top = top - under * xs[k]
            low = low - under * ys[k]
        for r in range(g + 1, near):
            ls = cols[r]
            for k in range(SUB):
                ls[k] = ls[k] * inv[k]
                for j in range(k + 1, SUB):
                    ls[j] = ls[j] - below[j][k] * ls[k]
                left[r] = left[r] - ls[k] * xs[k]
                right[r] = right[r] - ls[k] * ys[k]
        scale = inv[0]
        for k in range(1, SUB):
            scale = jnp.where(sub == k, inv[k], scale)
        top, low = top * scale, low * scale
        if near < groups:
            delta = far_product(top, jnp.concatenate([top, low], 1))
            for r in range(near, groups):
                left[r] = left[r] - delta[SUB * r : SUB * (r + 1), :size]
                right[r] = right[r] - delta[SUB * r : SUB * (r + 1), size:]
        tops.append(jnp.where(lane >= sub + SUB * g, top, 0.0))
        lows.append(low)
    return jnp.concatenate(tops, 0), jnp.concatenate(lows, 0)


def run_panels(lo, hi, row_of, r_ref, t_ref):
    width = t_ref.shape[1]
    start = lo * width

    row = row_of(lo)
    for k in range(hi - lo):
        at, end = k * width, (k + 1) * width
        if lo + k + 1 < hi:
            following = row_of(lo + k + 1)
            if k:
                following = following - dot_tn(r_ref[0:at, end : end + width], r_ref[0:at, end:])
        upper, inverse = diag_factor(row[:, :width])
        t_ref[at:end, :] = inverse
        r_ref[at:end, at:end] = upper
        if lo + k + 1 < hi:
            near = dot_nn(inverse, row[:, width : 2 * width])
            r_ref[at:end, end : end + width] = near
            block = following[:, :width] - dot_tn(near, near)
            far = dot_nn(inverse, row[:, 2 * width :])
            r_ref[at:end, end + width :] = far
            row = jnp.concatenate([block, following[:, width:] - dot_tn(near, far)], 1)
        else:
            r_ref[at:end, end:] = dot_nn(inverse, row[:, width:])


def stage_kernel(count, lo, hi, place_ref, own_ref, other_ref, *refs):
    refs = list(refs)
    before = lo > 0
    last = hi == count
    carry_ref = refs.pop(0) if before else None
    if last:
        earlier = [(refs.pop(0), refs.pop(0)) for _ in range((len(refs) - 5) // 2)]
        rows_ref, est_ref, r_ref, t_ref = refs[:4]
    else:
        r_ref, t_ref, left_ref = refs[:3]
    x_ref = refs[-1]
    width = x_ref.shape[1]
    states = count * width
    kept = upper_blocks(lo, hi, count)
    half = own_ref.shape[0]
    upper = place_ref[2 + CUT_PLACES.index(lo)]
    x_ref[pl.ds(pl.multiple_of(upper * half, SUB), half), :] = own_ref[...]
    x_ref[pl.ds(pl.multiple_of((1 - upper) * half, SUB), half), :] = other_ref[...]

    def taken_before(k):
        return carry_ref[(k - lo) * width : (k - lo + 1) * width, (k - lo) * width :]

    def vec_column(k):
        base = len(kept) * width
        return column_of(x_ref[base + k : base + k + 1, :])

    def row_of(k):
        parts = [x_ref[pl.ds(kept.index((k, j)) * width, width), :] for j in range(k, count)]
        if before:
            parts.append(jnp.zeros((width, width), F32))
            return jnp.concatenate(parts, 1) + taken_before(k)
        return jnp.concatenate(parts + [vec_column(k)], 1)

    run_panels(lo, hi, row_of, r_ref, t_ref)
    if not last:
        for k in range(hi, count):
            at = (k - lo) * width
            taken = dot_tn(r_ref[:, at : at + width], r_ref[:, at:])
            rows = slice((k - hi) * width, (k - hi + 1) * width)
            if before:
                left_ref[rows, (k - hi) * width :] = taken_before(k) - taken
            else:
                end = states - k * width
                left_ref[rows, (k - hi) * width : states - hi * width] = -taken[:, :end]
                left_ref[rows, states - hi * width :] = vec_column(k) - taken[:, end:]
        return

    owners = []
    groups = []
    for r, t in earlier + [(r_ref, t_ref)]:
        groups.append((r, t, len(owners)))
        owners += [groups[-1]] * (t.shape[0] // width)
    taken = [jnp.zeros((width, width), F32)] * count
    for k in reversed(range(count)):
        r, t, first = owners[k]
        mine = slice((k - first) * width, (k - first + 1) * width)
        right = r[mine, states - first * width :] - jnp.sum(taken[k], axis=1, keepdims=True)
        solved = jnp.sum(t[mine, :] * right, axis=0, keepdims=True)
        cols = slice(k * width, (k + 1) * width)
        est_ref[:, cols] = solved
        for i in range(k):
            r, t, first = owners[i]
            rows = slice((i - first) * width, (i - first + 1) * width)
            taken[i] = taken[i] + r[rows, (k - first) * width : (k - first + 1) * width] * solved
    share = rows_ref.shape[0]
    mine = place_ref[0] * share
    for r, t, first in groups:
        inside = jnp.logical_and(mine >= first * width, mine < first * width + t.shape[0])

        @pl.when(inside)
        def _(r=r, first=first):
            at = pl.multiple_of(mine - first * width, SUB)
            if first:
                rows_ref[:, : first * width] = jnp.zeros((share, first * width), F32)
            for j in range(first, count):
                cols = slice(j * width, (j + 1) * width)
                row = r[pl.ds(at, share), (j - first) * width : (j - first + 1) * width]
                rows_ref[:, cols] = jnp.where(mine < (j + 1) * width, row, 0.0)


def factor_stage(span, place, halves, carry, earlier, count, share):
    lo, hi = span
    width = halves[0].shape[1]
    states = count * width
    rest = states - lo * width
    rows = (hi - lo) * width
    last = hi == count
    vmem = pl.BlockSpec(memory_space=pltpu.VMEM)
    operands = list(halves)
    if lo:
        operands.append(carry)
    parts = [(rows, rest + width), (rows, width)]
    if last:
        operands += [x for pair in earlier for x in pair]
        outs = [(share, states), (1, states)]
    else:
        outs = parts + [(states - hi * width, states - hi * width + width)]
    scratch = (parts if last else []) + [(2 * halves[0].shape[0], width)]
    return pl.pallas_call(
        functools.partial(stage_kernel, count, lo, hi),
        in_specs=[pl.BlockSpec(memory_space=pltpu.SMEM)] + [vmem] * len(operands),
        out_specs=[vmem] * len(outs),
        out_shape=[jax.ShapeDtypeStruct(shape, F32) for shape in outs],
        scratch_shapes=[pltpu.VMEM(shape, F32) for shape in scratch],
        compiler_params=pltpu.CompilerParams(vmem_limit_bytes=FACTOR_VMEM_BYTES),
        cost_estimate=pl.CostEstimate(
            flops=(hi - lo) * FACTOR_FLOPS, bytes_accessed=8 * halves[0].size, transcendentals=rows
        ),
        name="factor",
    )(place, *operands)


def exchange(x, axis, mask):
    return lax.ppermute(x, axis, [(i, i ^ mask) for i in range(lax.axis_size(axis))])


def after(x, other):
    return lax.optimization_barrier((x, other))[0]


def is_upper(axis, bit):
    return ((lax.axis_index(axis) & bit) != 0).astype(jnp.int32)


def halve(x, axis, bit):
    half = x.shape[0] // 2
    upper = is_upper(axis, bit)
    return (
        lax.dynamic_slice_in_dim(x, upper * half, half, 0),
        lax.dynamic_slice_in_dim(x, (1 - upper) * half, half, 0),
    )


def per_device(values, blocks, noise_scale, readings, available, decay, prior_factor, prior_target):
    states = prior_factor.shape[0]
    width = values.shape[1] // 2
    count = states // width
    sensors = lax.axis_size("sensor")
    steps = lax.axis_size("tm")
    share = states // sensors
    own = lax.axis_index("sensor").astype(jnp.int32)
    time = lax.axis_index("tm")
    bits = [1 << n for n in range(sensors.bit_length() - 1)]
    turned = [bits[1], bits[0]] + bits[2:]
    spans = list(zip((0,) + CUTS, CUTS + (count,)))
    orders = [turned if n in TURNED else bits for n in range(len(spans))]
    uppers = [is_upper("sensor", order[0]) for order in orders]
    begins = (time == 0).astype(jnp.int32)

    def earlier(x, by):
        return lax.ppermute(x, "tm", [(i, i + by) for i in range(steps - by)])

    rest = (values, blocks.T, noise_scale, readings, available, prior_factor, prior_target)
    sizes = [packed_rows(lo, hi, count, width, sensors) for lo, hi in spans]
    offsets = [
        sum(is_upper("sensor", bit) * (size >> (n + 1)) for n, bit in enumerate(order))
        for size, order in zip(sizes, orders)
    ]
    place = jnp.stack([own, begins] + uppers + offsets)
    halves = list(local_gram(spans[:1], 0, place, *rest, count, sensors))
    later, halves[1] = lax.optimization_barrier((place, halves[1]))
    halves += local_gram(spans[1:], 1, later, *rest, count, sensors)
    own_decay = decay_pieces(place, decay, spans, count, width, sensors)
    decay = after(decay, halves[-1])
    shifted = {gap: earlier(decay, gap) for gap in range(1, steps // 2)}

    parts = []

    def stage(step):
        moved = [step(n, part) for n, part in enumerate(parts)]
        for n, (other, combine) in enumerate(moved):
            parts[n] = combine(other)

    def sum_first(n, part):
        return exchange(halves[2 * n + 1], "sensor", orders[n][0]), lambda other: part + other

    def sum_at(level):
        def step(n, part):
            stays, leaves = halve(part, "sensor", orders[n][level])
            return exchange(leaves, "sensor", orders[n][level]), lambda other: stays + other

        return step

    def add_earlier(by):
        between = 1.0
        for gap in range(1, by):
            between = between * shifted[gap]
        decays = decay_pieces(place, between, spans, count, width, sensors) if by > 1 else None

        def step(n, part):
            other = earlier(part * own_decay[n], by)
            if by > 1:
                other = other * decays[n]
            return other, lambda other: part + other

        return step

    def gather_at(level):
        def step(n, part):
            bit = orders[n][level]

            def combine(other):
                return jnp.where(
                    is_upper("sensor", bit) == 1,
                    jnp.concatenate([other, part], 0),
                    jnp.concatenate([part, other], 0),
                )

            return exchange(part, "sensor", bit), combine

        return step

    parts = halves[0::2]
    stage(sum_first)

    stage(sum_at(1))

    for level in range(2, len(bits)):
        stage(sum_at(level))
    by = 1
    while by < steps:
        stage(add_earlier(by))
        by *= 2
    for level in reversed(range(1, len(bits))):
        stage(gather_at(level))
    stage(lambda n, part: (exchange(part, "sensor", orders[n][0]), lambda other: (part, other)))
    done = []
    carry = None
    for span, pieces in zip(spans[:-1], parts):
        upper, inverses, carry = factor_stage(span, place, pieces, carry, [], count, share)
        done.append((upper, inverses))
    rows, estimate = factor_stage(spans[-1], place, parts[-1], carry, done, count, share)
    return rows[None], estimate


def solution(mesh):
    placed = (
        P("sensor", None),
        P("sensor", None),
        P("tm", "sensor"),
        P("tm", "sensor"),
        P("tm", "sensor"),
        P("tm", None),
        P(),
        P(),
    )
    return jax.shard_map(
        per_device,
        mesh=mesh,
        in_specs=placed,
        out_specs=(P("tm", "sensor", None), P("tm", None)),
        check_vma=False,
    )
```
